512 devices in a mesh: layer: 16 (over z, x_lo), dp: 32 (over x_hi, y, core).
Axes of the slice: x: 4 (x_hi: 2, x_lo: 2; x = x_hi * 2 + x_lo), y: 8, z: 8, core: 2. Of those that a mesh axis runs over, the one named last changes fastest.
Arguments:
- training_inputs: bfloat16 [16, 8192, 4096], P('layer', 'dp')
- training_output_gradient: bfloat16 [16, 8192, 4096], P('layer', 'dp')
- token_example_number: int32 [32, 256], P('dp'), may hold values from 0 to 31, never falling along the last dimension, each value on 1 to 16 neighbouring positions
- query_input_gradient: bfloat16 [16, 32, 2, 8, 4096], P('layer', 'dp'), may hold values from -6 to 6
- adapter_down_factor: bfloat16 [16, 16, 4096], P('layer')
- adapter_up_transposed: bfloat16 [16, 16, 4096], P('layer')
Outputs:
- scores: float32 [1024, 32], P('dp', 'layer')
The draws below stay inside these ranges and needn't reach their ends.
Inputs may be any that keep to these rules, and one draw needn't show every extreme that they name: `token_example_number`: within each block the example numbers never fall, every example 0 to 31 holds 1 to 16 tokens, and some example holds exactly 16.
All inputs are finite; a program needn't handle non-finite values.
Results may differ from the reference program's by a relative error of at most 0.0092.
Values may be sent and summed in bfloat16 or wider, within the bound.
A program may use at most 128 MiB of HBM per device.

```python
import math
import jax
import jax.numpy as jnp
import numpy as np
from jax import lax

D = 4096
RANK = 16
TOK_DEV = 256
EX_DEV = 32
Q_TOK = 8
LAYERS = 16
TOKENS = 8192
EXAMPLES = 1024
QUERIES = 32
N_DP = 32


def row_factors(key, spread):
    position = jnp.arange(TOKENS, dtype=jnp.float32) / max(TOKENS - 1, 1)
    rising = jnp.exp(math.log(3.0) * position)
    jitter = jnp.exp(jax.random.uniform(key, (LAYERS, TOKENS, 1), minval=0.0, maxval=math.log(spread)))
    return rising[None, :, None] * jitter


def draw_training_inputs(key, part):
    key = jax.random.fold_in(key, 11)
    key_base, key_row = jax.random.split(key, 2)
    base = jax.random.normal(key_base, (LAYERS, TOKENS, D))
    factors = row_factors(key_row, 3.0) / 3.0
    return (base * factors).astype(jnp.bfloat16)


def draw_training_output_gradient(key, part):
    key = jax.random.fold_in(key, 12)
    key_base, key_row = jax.random.split(key, 2)
    base = jax.random.normal(key_base, (LAYERS, TOKENS, D))
    factors = row_factors(key_row, 3.0) / 3.0
    return (base * factors).astype(jnp.bfloat16)


def adapter_factor(key):
    key_own, key_common = jax.random.split(key, 2)
    own = jax.random.normal(key_own, (LAYERS, RANK, D))
    common = jax.random.normal(key_common, (LAYERS, 1, D))
    return ((own + 0.7 * common) / math.sqrt(1.49 * D)).astype(jnp.bfloat16)


def draw_adapter_down_factor(key, part):
    key = jax.random.fold_in(key, 21)
    return adapter_factor(key)


def draw_adapter_up_transposed(key, part):
    key = jax.random.fold_in(key, 22)
    return adapter_factor(key)


def levels(rng, dims, cuts, low, top_value):
    factor_of = 1.0
    for dim, shards_of in cuts:
        steps = jax.random.uniform(jax.random.fold_in(jax.random.fold_in(rng, 6), dim), (shards_of,), jnp.float32, low / len(cuts), top_value / len(cuts))
        factor_of = factor_of * jnp.repeat(jnp.exp(steps), dims[dim] // shards_of).reshape((-1,) + (1,) * (len(dims) - 1 - dim))
    return factor_of


def split_up(count, total, most, lean):
    portions = [(1 << 20) // math.isqrt(rank ** lean) + 1 for rank in range(2, count + 1)]
    surplus, holding = total - most - (count - 1), [1] * (count - 1)
    while surplus > 0:
        candidates = [i for i in range(count - 1) if holding[i] < most]
        whole, budget = sum([portions[i] for i in candidates]), surplus
        for i in candidates:
            addition = min(most - holding[i], max(1, budget * portions[i] // whole), surplus)
            holding[i] = holding[i] + addition
            surplus = surplus - addition
    return np.array([most] + holding)


def uneven_parts(stream_key, number_of, total, most, skew):
    if number_of == 2:
        one = jax.random.randint(stream_key, (), max(1, total - most), min(most, total - 1) + 1)
        return jnp.stack([one, total - one])
    lengths = jnp.asarray(split_up(number_of, total, most, skew), jnp.int32)
    couples = (number_of - 1) // 2
    donor, taker = lengths[1:1 + 2 * couples:2], lengths[2:2 + 2 * couples:2]
    room = jnp.minimum(donor - 1, most - taker)
    moved = jax.random.randint(jax.random.fold_in(stream_key, 1), (couples,), 0, 1 << 20) % (room + 1)
    lengths = lengths.at[1:1 + 2 * couples:2].set(donor - moved).at[2:2 + 2 * couples:2].set(taker + moved)
    return lengths[jax.random.permutation(jax.random.fold_in(stream_key, 2), number_of)]


def scatter_about(stream_key, shape, width, bound, shards=(), kind=jnp.bfloat16):
    loudness = levels(stream_key, shape, shards, -0.22, 0.18) if shards else 1.0
    array = jax.random.normal(stream_key, shape, jnp.float32) * width * loudness
    return jnp.minimum(jnp.maximum(array, -bound), bound).astype(kind)


def setup_inputs(seed: int = 0) -> dict:
    streams_of = jax.random.split(jax.random.key(seed), 7)
    training_inputs = draw_training_inputs(jax.random.fold_in(streams_of[6], 71), 0)
    training_output_gradient = draw_training_output_gradient(jax.random.fold_in(streams_of[6], 71), 0)
    token_example_number = jax.vmap(lambda own: jnp.searchsorted(jnp.cumsum(uneven_parts(own, EX_DEV, TOK_DEV, 16, 1)), jnp.arange(TOK_DEV), side="right"))(jax.random.split(streams_of[2], N_DP)).reshape((N_DP, TOK_DEV)).astype(jnp.int32)
    query_input_gradient = scatter_about(streams_of[3], (LAYERS, QUERIES, 2, Q_TOK, D), 1.0, 6.0, ((0, 16), (1, 32)))
    adapter_down_factor = draw_adapter_down_factor(jax.random.fold_in(streams_of[6], 71), 0)
    adapter_up_transposed = draw_adapter_up_transposed(jax.random.fold_in(streams_of[6], 71), 0)
    return {"training_inputs": training_inputs, "training_output_gradient": training_output_gradient, "token_example_number": token_example_number, "query_input_gradient": query_input_gradient, "adapter_down_factor": adapter_down_factor, "adapter_up_transposed": adapter_up_transposed}


def damped_factor(covariance):
    adapter_rank = covariance.shape[0]
    shift = 0.1 * jnp.trace(covariance) / adapter_rank
    return jnp.linalg.cholesky(covariance + shift * jnp.eye(adapter_rank, dtype=covariance.dtype))

def precondition(projected, lower_factor):
    solved = jax.scipy.linalg.cho_solve((lower_factor, True), projected.T)
    return solved.T.astype(jnp.bfloat16)

def reference(training_inputs, training_output_gradient, token_example_number, query_input_gradient, adapter_down_factor, adapter_up_transposed):
    highest = lax.Precision.HIGHEST

    def single_layer(layer_args):
        acts, grads, queries, down_factor_matrix, up_factor_transposed = layer_args
        grad_proj = jnp.dot(grads.astype(jnp.float32), up_factor_transposed.T.astype(jnp.float32), preferred_element_type=jnp.float32)
        act_proj = jnp.dot(acts.astype(jnp.float32), down_factor_matrix.T.astype(jnp.float32), preferred_element_type=jnp.float32)
        lower_grad = damped_factor(jnp.dot(grad_proj.T, grad_proj, precision=highest) / TOKENS)
        lower_act = damped_factor(jnp.dot(act_proj.T, act_proj, precision=highest) / TOKENS)
        query_acts = queries[:, 0]
        query_grads = queries[:, 1]
        query_gproj = jnp.dot(query_grads.reshape(QUERIES * Q_TOK, D).astype(jnp.float32), up_factor_transposed.T.astype(jnp.float32), preferred_element_type=jnp.float32)
        query_aproj = jnp.dot(query_acts.reshape(QUERIES * Q_TOK, D).astype(jnp.float32), down_factor_matrix.T.astype(jnp.float32), preferred_element_type=jnp.float32)
        weighted_grad = precondition(query_gproj, lower_grad).reshape(QUERIES, Q_TOK, RANK)
        weighted_act = precondition(query_aproj, lower_act).reshape(QUERIES, Q_TOK, RANK)
        formed_a = jnp.einsum('ktr,ktd->krd', weighted_grad.astype(jnp.float32), query_acts.astype(jnp.float32), precision=highest)
        formed_b = jnp.einsum('ktr,ktd->krd', weighted_act.astype(jnp.float32), query_grads.astype(jnp.float32), precision=highest)
        formed_a = formed_a.astype(jnp.bfloat16).astype(jnp.float32).reshape(QUERIES, RANK * D)
        formed_b = formed_b.astype(jnp.bfloat16).astype(jnp.float32).reshape(QUERIES, RANK * D)
        block_args = (acts.reshape(N_DP, TOK_DEV, D), grads.reshape(N_DP, TOK_DEV, D), grad_proj.astype(jnp.bfloat16).reshape(N_DP, TOK_DEV, RANK), act_proj.astype(jnp.bfloat16).reshape(N_DP, TOK_DEV, RANK), token_example_number)

        def one_block(block):
            block_acts, block_grads, block_gproj, block_aproj, members = block
            outer_a = block_gproj.astype(jnp.float32)[:, :, None] * block_acts.astype(jnp.float32)[:, None, :]
            grad_a = jax.ops.segment_sum(outer_a, members, num_segments=EX_DEV)
            grad_a = grad_a.astype(jnp.bfloat16).astype(jnp.float32).reshape(EX_DEV, RANK * D)
            outer_b = block_aproj.astype(jnp.float32)[:, :, None] * block_grads.astype(jnp.float32)[:, None, :]
            grad_b = jax.ops.segment_sum(outer_b, members, num_segments=EX_DEV)
            grad_b = grad_b.astype(jnp.bfloat16).astype(jnp.float32).reshape(EX_DEV, RANK * D)
            return jnp.dot(grad_a, formed_a.T, precision=highest) + jnp.dot(grad_b, formed_b.T, precision=highest)
        return lax.map(one_block, block_args).reshape(EXAMPLES, QUERIES)
    partial_scores = lax.map(single_layer, (training_inputs, training_output_gradient, query_input_gradient, adapter_down_factor, adapter_up_transposed))
    total = lax.optimization_barrier(jnp.sum(partial_scores, axis=0))
    return total / (8.0 * math.sqrt(2.0 * RANK * D * LAYERS))
```

```python
import math

import jax
import jax.numpy as jnp
from jax import lax
from jax.experimental import pallas as pl
from jax.experimental.pallas import tpu as pltpu
from jax.sharding import PartitionSpec as P

MESH = pl.DeviceIdType.MESH
F32 = jnp.float32
BF16 = jnp.bfloat16
HIGHEST = lax.Precision.HIGHEST
NT = (((1,), (1,)), ((), ()))
NN = (((1,), (0,)), ((), ()))

TOK = 256
WIDTH = 4096
HALF = WIDTH // 2
RANK = 16
TOKENS = 8192
ROWS = 16

GROUPS = (
    ((0, 0, 0), (0, 0, 1), (0, 1, 0), (0, -1, 0), (0, 1, 1), (0, -1, 1), (1, 0, 0), (1, 0, 1)),
    ((0, 2, 0), (0, -2, 0), (0, 2, 1), (0, -2, 1), (1, 1, 0), (1, -1, 0)),
    ((0, 3, 0), (0, -3, 0), (0, 3, 1), (0, -3, 1), (1, 2, 0), (1, -2, 0), (1, 1, 1), (1, -1, 1)),
    ((0, 4, 0), (0, 4, 1), (1, 2, 1), (1, -2, 1), (1, 3, 0), (1, 3, 1)),
    ((1, -3, 0), (1, -3, 1), (1, 4, 0), (1, 4, 1)),
)
ORDER = tuple(piece for group in GROUPS for piece in group)
POS = {piece: i for i, piece in enumerate(ORDER)}
SLOTS = tuple((dx, d) for dx in (0, 1) for d in (0, 1, -1, 2, -2, 3, -3, 4))
SLOT = {slot: i for i, slot in enumerate(SLOTS)}

ONWARD = {
    (0, 0, 0): "+-x", (0, 0, 1): "+-x",
    (0, 1, 0): "+x", (0, 1, 1): "+", (0, -1, 0): "-x", (0, -1, 1): "-",
    (0, 2, 0): "+x", (0, 2, 1): "+", (0, -2, 0): "-x", (0, -2, 1): "-",
    (0, 3, 0): "x", (0, 3, 1): "x", (0, -3, 0): "-x", (0, -3, 1): "-x",
    (1, 0, 1): "+-", (1, 1, 1): "+", (1, -1, 1): "-",
    (1, 3, 0): "+", (1, 3, 1): "+",
}


def moved(piece, way):
    dx, d, p = piece
    if way == "x":
        return (1 - dx, d, p)
    d = d + 1 if way == "+" else d - 1
    return (dx, 4 if d == -4 else d, p)


def dot(a, b, dims, precision=None):
    return lax.dot_general(a, b, dims, precision=precision, preferred_element_type=F32)


def kernel(
    x_ref, g_ref, member_ref, query_ref, down_ref, up_ref, out_ref,
    xb, gb, xo, go, fm, fo, q, qo, mine, theirs, pm, ps, pown, psib,
    work, rall, vb, kst, onehot, so, rx,
    load_sem, piece_sem, send_sem, side_send, side_recv, msg_send, msg_recv, fin_send, fin_recv, known,
):
    layer, block = lax.axis_index("layer"), lax.axis_index("dp")
    xh, y, core = block // 16, (block // 2) % 8, block % 2
    z, xl = layer // 2, layer % 2

    def along_y(n):
        return (layer, xh * 16 + ((y + n + 8) % 8) * 2 + core)

    def along_z(n):
        return (((z + n + 8) % 8) * 2 + xl, block)

    partner = (layer, (1 - xh) * 16 + y * 2 + core)
    sibling = (layer, xh * 16 + y * 2 + (1 - core))
    beside = (z * 2 + (1 - xl), block)
    ways = {"+": along_y(1), "-": along_y(-1), "x": partner}

    def remote(src, dst, ssem, rsem, device):
        return pltpu.make_async_remote_copy(
            src_ref=src, dst_ref=dst, send_sem=ssem, recv_sem=rsem, device_id=device, device_id_type=MESH
        )

    def signal(sem, device):
        pl.semaphore_signal(sem, inc=1, device_id=device, device_id_type=MESH)

    def rows(piece):
        return pl.ds(POS[piece] * ROWS, ROWS)

    here = pl.ds(pl.multiple_of(core * HALF, HALF), HALF)
    there = pl.ds(pl.multiple_of((1 - core) * HALF, HALF), HALF)

    near = (
        along_y(1), along_y(-1), along_y(2), along_y(-2), partner, sibling,
        beside, along_z(1), along_z(-1), along_z(2), along_z(-2),
    )
    barrier = pltpu.get_barrier_semaphore()
    for device in near:
        signal(barrier, device)

    loads = [
        pltpu.make_async_copy(query_ref.at[:, here], q.at[rows((0, 0, 0))], load_sem.at[0]),
        pltpu.make_async_copy(query_ref.at[:, there], qo, load_sem.at[1]),
        pltpu.make_async_copy(up_ref.at[0, :, here], fm.at[pl.ds(0, RANK)], load_sem.at[2]),
        pltpu.make_async_copy(up_ref.at[0, :, there], fo.at[pl.ds(0, RANK)], load_sem.at[3]),
        pltpu.make_async_copy(down_ref.at[0, :, here], fm.at[pl.ds(RANK, RANK)], load_sem.at[4]),
        pltpu.make_async_copy(down_ref.at[0, :, there], fo.at[pl.ds(RANK, RANK)], load_sem.at[5]),
        pltpu.make_async_copy(g_ref.at[0, :, here], gb.at[pl.ds(0, TOK)], load_sem.at[6]),
        pltpu.make_async_copy(g_ref.at[0, :, there], go, load_sem.at[7]),
        pltpu.make_async_copy(x_ref.at[0, :, here], xb.at[pl.ds(0, TOK)], load_sem.at[8]),
        pltpu.make_async_copy(x_ref.at[0, :, there], xo, load_sem.at[9]),
    ]
    for copy in loads:
        copy.start()
    for copy in loads[:6]:
        copy.wait()
    own_q = dot(fm[...], q[pl.ds(0, ROWS), :], NT) + dot(fo[...], qo[...], NT)
    query_proj = jnp.concatenate([own_q[0:RANK, 8:16], own_q[RANK:, 0:8]], axis=1)
    loads[6].wait()
    loads[7].wait()
    gproj = dot(fm[0:RANK, :], gb[0:TOK, :], NT) + dot(fo[0:RANK, :], go[...], NT)
    loads[8].wait()
    loads[9].wait()
    aproj = dot(fm[RANK:, :], xb[0:TOK, :], NT) + dot(fo[RANK:, :], xo[...], NT)
    proj = jnp.concatenate([gproj, aproj], axis=0)
    cov = dot(proj, proj, NT, HIGHEST)
    both = jnp.concatenate(
        [cov[0:RANK, 0:RANK], cov[RANK:, RANK:], query_proj, jnp.zeros((RANK, 16), F32)], axis=1
    )
    mine[...] = jnp.concatenate([both[0:8], both[8:16]], axis=1)
    members = member_ref[...]
    pown[0:32, :] = proj.astype(BF16)
    pown[32:48, :] = jnp.broadcast_to(members.astype(F32), (16, TOK)).astype(BF16)
    so[...] = jnp.zeros(so.shape, F32)

    pl.semaphore_wait(barrier, len(near))

    def onward(piece):
        for way in ONWARD.get(piece, ""):
            remote(
                q.at[rows(piece)], q.at[rows(moved(piece, way))], send_sem, piece_sem.at[POS[moved(piece, way)]], ways[way]
            ).start()

    def landed(*pieces):
        for piece in pieces:
            remote(
                q.at[rows(piece)], q.at[rows(piece)], send_sem, piece_sem.at[POS[piece]], partner
            ).wait_recv()
            onward(piece)

    to_partner = remote(mine, theirs, msg_send.at[0], msg_recv.at[0], partner)
    to_partner.start()
    onward((0, 0, 0))
    side = [
        remote(qo, q.at[rows((0, 0, 1))], side_send.at[0], piece_sem.at[POS[(0, 0, 1)]], sibling),
        remote(pown, psib, side_send.at[1], side_recv.at[1], sibling),
        remote(go, gb.at[pl.ds(TOK, TOK)], side_send.at[2], side_recv.at[2], sibling),
        remote(xo, xb.at[pl.ds(TOK, TOK)], side_send.at[3], side_recv.at[3], sibling),
    ]
    for copy in side:
        copy.start()
    for device in (along_y(2), along_y(-2), along_z(2), along_z(-2)):
        signal(known.at[0], device)
    landed((0, 0, 1))

    pl.semaphore_wait(known.at[0], 4)
    signal(known.at[1], beside)
    to_partner.wait_recv()
    lane = lax.broadcasted_iota(jnp.int32, (8, 128), 1) % 64
    from_x = theirs[...]
    own = mine[...]
    pm[0] = jnp.where(lane < 32, own + from_x, jnp.where(lane < 48, own, pltpu.roll(from_x, 16, 1)))
    pair = [remote(pm.at[0], pm.at[n], msg_send.at[1], msg_recv.at[1], along_y(n)) for n in range(1, 8)]
    for copy in pair:
        copy.start()

    landed((0, 1, 0), (0, -1, 0), (1, 0, 0), (0, 1, 1), (0, -1, 1), (1, 0, 1))

    pl.semaphore_wait(known.at[1], 1)
    signal(known.at[2], sibling)
    side[1].wait_recv()
    side[2].wait_recv()
    side[3].wait_recv()

    def products(index):
        group = GROUPS[index]
        first = POS[group[0]] * ROWS
        count = len(group) * ROWS
        block_rows = q[first:first + count, :]
        with_x = dot(block_rows, xb[...], NT)
        with_g = dot(block_rows, gb[...], NT)
        for i in range(0, count, ROWS):
            kst[first + i:first + i + 8, :] = with_x[i:i + 8]
            kst[first + i + 8:first + i + 16, :] = with_g[i + 8:i + 16]

    def scores(index):
        group = GROUPS[index]
        first = POS[group[0]] * ROWS
        count = len(group) * ROWS
        weights = dot(vb[first:first + count, :], pcat(), NN)
        terms = (weights * kst[first:first + count, :]).reshape(len(group), ROWS, 2 * TOK)
        terms = jnp.sum(terms, axis=1)
        high = terms.astype(BF16)
        low = (terms - high.astype(F32)).astype(BF16)
        sums = dot(high, onehot[...], NT) + dot(low, onehot[...], NT)
        for i, (dx, d, p) in enumerate(group):
            for k in (0, 1):
                so[SLOT[dx, d], k, p:p + 1, :] = sums[i:i + 1, k * 128:(k + 1) * 128]

    def pcat():
        return jnp.concatenate([pown[0:32, :], psib[0:32, :]], axis=1)

    def send_scores(index):
        done = {piece for group in GROUPS[:index + 1] for piece in group}
        before = {piece for group in GROUPS[:index] for piece in group}
        for slot in SLOTS:
            pieces = {slot + (0,), slot + (1,)}
            if not pieces <= done or pieces <= before:
                continue
            dx, d = slot
            target = ((1 - xh) if dx else xh) * 8 + (y - d + 8) % 8
            step = (target - layer + 16) % 16
            mate = xh * 16 + y * 2 + (1 - core)

            @pl.when(step == 0)
            def _():
                rx[0] = so[SLOT[slot], 0]

            @pl.when(step != 0)
            def _():
                remote(so.at[SLOT[slot], 0], rx.at[step * 2], fin_send, fin_recv, (target, block)).start()

            remote(so.at[SLOT[slot], 1], rx.at[step * 2 + 1], fin_send, fin_recv, (target, mate)).start()

    example = lax.broadcasted_iota(jnp.int32, (128, TOK), 0)
    onehot[0:128, 0:TOK] = (example == members).astype(F32).astype(BF16)
    onehot[0:128, TOK:] = jnp.zeros((128, TOK), BF16)
    onehot[128:, 0:TOK] = jnp.zeros((128, TOK), BF16)
    others = psib[32:48, :].astype(F32)[0:1, :]
    onehot[128:, TOK:] = (example.astype(F32) == others).astype(F32).astype(BF16)

    products(0)
    landed((0, 2, 0), (0, -2, 0), (1, 1, 0), (1, -1, 0), (0, 2, 1), (0, -2, 1), (1, 1, 1), (1, -1, 1))

    remote(pm.at[pl.ds(1, 7)], pm.at[pl.ds(1, 7)], msg_send.at[1], msg_recv.at[1], sibling).wait_recv()
    across = remote(pm, ps, msg_send.at[2], msg_recv.at[2], sibling)
    across.start()
    products(1)
    landed((0, 3, 0), (0, -3, 0))

    across.wait_recv()
    total = pm[0] + ps[0]
    for n in range(1, 8):
        total = total + (pm[n] + ps[n])
    moments = jnp.concatenate([total[:, 0:32], total[:, 64:96]], axis=0) * (1.0 / TOKENS)
    for i, (dx, d, p) in enumerate(ORDER):
        source = (ps if p else pm)[(d + 8) % 8]
        at = 32 + 16 * dx
        rall[0:8, 16 * i:16 * i + 16] = source[:, at:at + 16]
        rall[8:16, 16 * i:16 * i + 16] = source[:, at + 64:at + 80]
    diagonal = (
        lax.broadcasted_iota(jnp.int32, (RANK, RANK), 0) == lax.broadcasted_iota(jnp.int32, (RANK, RANK), 1)
    ).astype(F32)
    scales = []
    for i in (0, 1):
        part = moments[:, RANK * i:RANK * (i + 1)]
        trace = jnp.sum(jnp.sum(part * diagonal, axis=1, keepdims=True), axis=0, keepdims=True)
        scale = 1.0 / trace
        scales.append(scale)
        work[i] = jnp.concatenate([part * scale + (0.1 / RANK) * diagonal, diagonal], axis=1)

    def eliminate(begin, end):
        row = lax.broadcasted_iota(jnp.int32, (RANK, 2 * RANK), 0)
        tables = [work[0], work[1]]
        for k in range(begin, end):
            for i in (0, 1):
                table = tables[i]
                pivot = table[k:k + 1, :] / table[k:k + 1, k:k + 1]
                tables[i] = jnp.where(row == k, pivot, table - table[:, k:k + 1] * pivot)
        work[0] = tables[0]
        work[1] = tables[1]

    landed((0, 3, 1), (0, -3, 1))
    eliminate(0, 4)
    landed((1, 2, 0), (1, -2, 0))
    eliminate(4, 8)
    landed((1, 2, 1), (1, -2, 1))
    eliminate(8, 12)
    landed((1, 3, 0))
    eliminate(12, 16)
    landed((1, 3, 1))
    kind = lax.broadcasted_iota(jnp.int32, (RANK, 32 * ROWS), 1) % ROWS
    solved_grad = dot(work[0][:, RANK:], rall[...] * scales[0], NN, HIGHEST)
    solved_act = dot(work[1][:, RANK:], rall[...] * scales[1], NN, HIGHEST)
    solved = jnp.concatenate(
        [jnp.where(kind < 8, solved_grad, 0.0), jnp.where(kind < 8, 0.0, solved_act)], axis=0
    )
    vb[...] = solved.T.astype(BF16)
    pl.semaphore_wait(known.at[2], 1)
    products(2)
    for index in (0, 1, 2):
        scores(index)
        send_scores(index)
    landed((0, 4, 0), (0, 4, 1))
    products(3)
    scores(3)
    send_scores(3)
    landed((1, -3, 0), (1, -3, 1), (1, 4, 0), (1, 4, 1))
    products(4)
    scores(4)
    send_scores(4)

    tail = rx.at[pl.ds(1, 31)]
    remote(tail, tail, fin_send, fin_recv, sibling).wait()
    same, other = rx[0], rx[1]
    for i in range(1, 16):
        same = same + rx[2 * i]
        other = other + rx[2 * i + 1]
    first = same[0:1, 0:32] + other[1:2, 0:32]
    second = same[1:2, 0:32] + other[0:1, 0:32]
    scale = 1.0 / (8.0 * math.sqrt(2.0 * RANK * WIDTH * 16))
    out_ref[0:1, :] = jnp.where(core == 0, first, second) * scale
    out_ref[1:2, :] = jnp.where(core == 0, second, first) * scale

    sent = q.at[pl.ds(0, 30 * ROWS)]
    remote(sent, sent, send_sem, piece_sem.at[0], partner).wait_send()
    for copy in side:
        copy.wait_send()
    to_partner.wait_send()
    remote(pm.at[pl.ds(1, 7)], pm.at[pl.ds(1, 7)], msg_send.at[1], msg_recv.at[1], sibling).wait_send()
    across.wait_send()


def local(x, g, members, queries, down, up):
    anywhere = pl.BlockSpec(memory_space=pl.ANY)
    vmem = pl.BlockSpec(memory_space=pltpu.VMEM)
    dma = pltpu.SemaphoreType.DMA
    out = pl.pallas_call(
        kernel,
        out_shape=jax.ShapeDtypeStruct((2, 32), F32),
        in_specs=[anywhere, anywhere, vmem, anywhere, anywhere, anywhere],
        out_specs=vmem,
        scratch_shapes=[
            pltpu.VMEM((2 * TOK, HALF), BF16),
            pltpu.VMEM((2 * TOK, HALF), BF16),
            pltpu.VMEM((TOK, HALF), BF16),
            pltpu.VMEM((TOK, HALF), BF16),
            pltpu.VMEM((2 * RANK, HALF), BF16),
            pltpu.VMEM((2 * RANK, HALF), BF16),
            pltpu.VMEM((32 * ROWS, HALF), BF16),
            pltpu.VMEM((ROWS, HALF), BF16),
            pltpu.VMEM((8, 128), F32),
            pltpu.VMEM((8, 128), F32),
            pltpu.VMEM((8, 8, 128), F32),
            pltpu.VMEM((8, 8, 128), F32),
            pltpu.VMEM((48, TOK), BF16),
            pltpu.VMEM((48, TOK), BF16),
            pltpu.VMEM((2, RANK, 2 * RANK), F32),
            pltpu.VMEM((RANK, 32 * ROWS), F32),
            pltpu.VMEM((32 * ROWS, 2 * RANK), BF16),
            pltpu.VMEM((32 * ROWS, 2 * TOK), F32),
            pltpu.VMEM((256, 2 * TOK), BF16),
            pltpu.VMEM((16, 2, 8, 128), F32),
            pltpu.VMEM((32, 8, 128), F32),
            dma((10,)),
            dma((32,)),
            dma,
            dma((4,)),
            dma((4,)),
            dma((3,)),
            dma((3,)),
            dma,
            dma,
            pltpu.SemaphoreType.REGULAR((3,)),
        ],
        compiler_params=pltpu.CompilerParams(
            collective_id=0, has_side_effects=True, vmem_limit_bytes=48 * 1024 * 1024
        ),
        name="influence",
    )(x, g, members, queries.reshape(ROWS, WIDTH), down, up)
    return out.T


def solution(mesh):
    placed = (
        P("layer", "dp", None),
        P("layer", "dp", None),
        P("dp", None),
        P("layer", "dp", None, None, None),
        P("layer", None, None),
        P("layer", None, None),
    )
    return jax.shard_map(
        local, mesh=mesh, in_specs=placed, out_specs=P("dp", "layer"), check_vma=False
    )
```

```python
import math

import jax
import jax.numpy as jnp
from jax import lax
from jax.experimental import pallas as pl
from jax.experimental.pallas import tpu as pltpu
from jax.sharding import PartitionSpec as P

MESH = pl.DeviceIdType.MESH
F32 = jnp.float32
BF16 = jnp.bfloat16
HIGHEST = lax.Precision.HIGHEST
NT = (((1,), (1,)), ((), ()))
NN = (((1,), (0,)), ((), ()))

TOK = 256
WIDTH = 4096
HALF = WIDTH // 2
RANK = 16
TOKENS = 8192
ROWS = 16

GROUPS = (
    ((0, 0, 0), (0, 0, 1), (0, 1, 0), (0, -1, 0), (0, 1, 1), (0, -1, 1), (1, 0, 0), (1, 0, 1)),
    ((0, 2, 0), (0, -2, 0), (0, 2, 1), (0, -2, 1), (1, 1, 0), (1, -1, 0)),
    ((0, 3, 0), (0, -3, 0), (0, 3, 1), (0, -3, 1), (1, 2, 0), (1, -2, 0), (1, 1, 1), (1, -1, 1)),
    ((0, 4, 0), (0, 4, 1), (1, 2, 1), (1, -2, 1), (1, 3, 0), (1, 3, 1)),
    ((1, -3, 0), (1, -3, 1), (1, 4, 0), (1, 4, 1)),
)
ORDER = tuple(piece for group in GROUPS for piece in group)
POS = {piece: i for i, piece in enumerate(ORDER)}
SLOTS = tuple((dx, d) for dx in (0, 1) for d in (0, 1, -1, 2, -2, 3, -3, 4))
SLOT = {slot: i for i, slot in enumerate(SLOTS)}

ONWARD = {
    (0, 0, 0): "+-x", (0, 0, 1): "+-x",
    (0, 1, 0): "+x", (0, 1, 1): "+", (0, -1, 0): "-x", (0, -1, 1): "-",
    (0, 2, 0): "+x", (0, 2, 1): "+", (0, -2, 0): "-x", (0, -2, 1): "-",
    (0, 3, 0): "x", (0, 3, 1): "x", (0, -3, 0): "-x", (0, -3, 1): "-x",
    (1, 0, 1): "+-", (1, 1, 1): "+", (1, -1, 1): "-",
    (1, 3, 0): "+", (1, 3, 1): "+",
}


def moved(piece, way):
    dx, d, p = piece
    if way == "x":
        return (1 - dx, d, p)
    d = d + 1 if way == "+" else d - 1
    return (dx, 4 if d == -4 else d, p)


def dot(a, b, dims, precision=None):
    return lax.dot_general(a, b, dims, precision=precision, preferred_element_type=F32)


def kernel(
    x_ref, g_ref, member_ref, query_ref, down_ref, up_ref, out_ref,
    xb, gb, xo, go, fm, fo, q, qo, mine, theirs, pm, ps, pown, psib,
    work, rall, vb, kst, onehot, so, rx,
    mem, load_sem, piece_sem, send_sem, side_send, side_recv, msg_send, msg_recv, fin_send, fin_recv, known,
):
    layer, block = lax.axis_index("layer"), lax.axis_index("dp")
    xh, y, core = block // 16, (block // 2) % 8, block % 2
    z, xl = layer // 2, layer % 2

    def along_y(n):
        return (layer, xh * 16 + ((y + n + 8) % 8) * 2 + core)

    def along_z(n):
        return (((z + n + 8) % 8) * 2 + xl, block)

    partner = (layer, (1 - xh) * 16 + y * 2 + core)
    sibling = (layer, xh * 16 + y * 2 + (1 - core))
    beside = (z * 2 + (1 - xl), block)
    ways = {"+": along_y(1), "-": along_y(-1), "x": partner}

    def remote(src, dst, ssem, rsem, device):
        return pltpu.make_async_remote_copy(
            src_ref=src, dst_ref=dst, send_sem=ssem, recv_sem=rsem, device_id=device, device_id_type=MESH
        )

    def signal(sem, device):
        pl.semaphore_signal(sem, inc=1, device_id=device, device_id_type=MESH)

    def rows(piece):
        return pl.ds(POS[piece] * ROWS, ROWS)

    here = pl.ds(pl.multiple_of(core * HALF, HALF), HALF)
    there = pl.ds(pl.multiple_of((1 - core) * HALF, HALF), HALF)

    near = (
        along_y(1), along_y(-1), along_y(2), along_y(-2), partner, sibling,
        beside, along_z(1), along_z(-1), along_z(2), along_z(-2),
    )
    barrier = pltpu.get_barrier_semaphore()
    for device in near:
        signal(barrier, device)

    loads = [
        pltpu.make_async_copy(query_ref.at[:, here], q.at[rows((0, 0, 0))], load_sem.at[0]),
        pltpu.make_async_copy(query_ref.at[:, there], qo, load_sem.at[1]),
        pltpu.make_async_copy(up_ref.at[0, :, here], fm.at[pl.ds(0, RANK)], load_sem.at[2]),
        pltpu.make_async_copy(up_ref.at[0, :, there], fo.at[pl.ds(0, RANK)], load_sem.at[3]),
        pltpu.make_async_copy(down_ref.at[0, :, here], fm.at[pl.ds(RANK, RANK)], load_sem.at[4]),
        pltpu.make_async_copy(down_ref.at[0, :, there], fo.at[pl.ds(RANK, RANK)], load_sem.at[5]),
        pltpu.make_async_copy(g_ref.at[0, :, here], gb.at[pl.ds(0, TOK)], load_sem.at[6]),
        pltpu.make_async_copy(g_ref.at[0, :, there], go, load_sem.at[7]),
        pltpu.make_async_copy(x_ref.at[0, :, here], xb.at[pl.ds(0, TOK)], load_sem.at[8]),
        pltpu.make_async_copy(x_ref.at[0, :, there], xo, load_sem.at[9]),
        pltpu.make_async_copy(member_ref, mem, load_sem.at[10]),
    ]
    for copy in loads:
        copy.start()
    for copy in loads[:6]:
        copy.wait()
    own_q = dot(fm[...], q[pl.ds(0, ROWS), :], NT) + dot(fo[...], qo[...], NT)
    query_proj = jnp.concatenate([own_q[0:RANK, 8:16], own_q[RANK:, 0:8]], axis=1)
    loads[6].wait()
    loads[7].wait()
    gproj = dot(fm[0:RANK, :], gb[0:TOK, :], NT) + dot(fo[0:RANK, :], go[...], NT)
    loads[8].wait()
    loads[9].wait()
    aproj = dot(fm[RANK:, :], xb[0:TOK, :], NT) + dot(fo[RANK:, :], xo[...], NT)
    proj = jnp.concatenate([gproj, aproj], axis=0)
    cov = dot(proj, proj, NT, HIGHEST)
    both = jnp.concatenate(
        [cov[0:RANK, 0:RANK], cov[RANK:, RANK:], query_proj, jnp.zeros((RANK, 16), F32)], axis=1
    )
    mine[...] = jnp.concatenate([both[0:8], both[8:16]], axis=1)
    loads[10].wait()
    members = mem[...]
    pown[0:32, :] = proj.astype(BF16)
    pown[32:48, :] = jnp.broadcast_to(members.astype(F32), (16, TOK)).astype(BF16)
    so[...] = jnp.zeros(so.shape, F32)

    pl.semaphore_wait(barrier, len(near))

    def onward(piece):
        for way in ONWARD.get(piece, ""):
            remote(
                q.at[rows(piece)], q.at[rows(moved(piece, way))], send_sem, piece_sem.at[POS[moved(piece, way)]], ways[way]
            ).start()

    def landed(*pieces):
        for piece in pieces:
            remote(
                q.at[rows(piece)], q.at[rows(piece)], send_sem, piece_sem.at[POS[piece]], partner
            ).wait_recv()
            onward(piece)

    to_partner = remote(mine, theirs, msg_send.at[0], msg_recv.at[0], partner)
    to_partner.start()
    onward((0, 0, 0))
    side = [
        remote(qo, q.at[rows((0, 0, 1))], side_send.at[0], piece_sem.at[POS[(0, 0, 1)]], sibling),
        remote(pown, psib, side_send.at[1], side_recv.at[1], sibling),
        remote(go, gb.at[pl.ds(TOK, TOK)], side_send.at[2], side_recv.at[2], sibling),
        remote(xo, xb.at[pl.ds(TOK, TOK)], side_send.at[3], side_recv.at[3], sibling),
    ]
    for copy in side:
        copy.start()
    for device in (along_y(2), along_y(-2), along_z(2), along_z(-2)):
        signal(known.at[0], device)
    landed((0, 0, 1))

    pl.semaphore_wait(known.at[0], 4)
    signal(known.at[1], beside)
    to_partner.wait_recv()
    lane = lax.broadcasted_iota(jnp.int32, (8, 128), 1) % 64
    from_x = theirs[...]
    own = mine[...]
    pm[0] = jnp.where(lane < 32, own + from_x, jnp.where(lane < 48, own, pltpu.roll(from_x, 16, 1)))
    pair = [remote(pm.at[0], pm.at[n], msg_send.at[1], msg_recv.at[1], along_y(n)) for n in range(1, 8)]
    for copy in pair:
        copy.start()

    landed((0, 1, 0), (0, -1, 0), (1, 0, 0), (0, 1, 1), (0, -1, 1), (1, 0, 1))

    pl.semaphore_wait(known.at[1], 1)
    signal(known.at[2], sibling)
    side[1].wait_recv()
    side[2].wait_recv()
    side[3].wait_recv()

    def products(index):
        group = GROUPS[index]
        first = POS[group[0]] * ROWS
        count = len(group) * ROWS
        block_rows = q[first:first + count, :]
        with_x = dot(block_rows, xb[...], NT)
        with_g = dot(block_rows, gb[...], NT)
        for i in range(0, count, ROWS):
            kst[first + i:first + i + 8, :] = with_x[i:i + 8]
            kst[first + i + 8:first + i + 16, :] = with_g[i + 8:i + 16]

    def scores(index):
        group = GROUPS[index]
        first = POS[group[0]] * ROWS
        count = len(group) * ROWS
        weights = dot(vb[first:first + count, :], pcat(), NN)
        terms = (weights * kst[first:first + count, :]).reshape(len(group), ROWS, 2 * TOK)
        terms = jnp.sum(terms, axis=1)
        high = terms.astype(BF16)
        low = (terms - high.astype(F32)).astype(BF16)
        sums = dot(high, onehot[...], NT) + dot(low, onehot[...], NT)
        for i, (dx, d, p) in enumerate(group):
            for k in (0, 1):
                so[SLOT[dx, d], k, p:p + 1, :] = sums[i:i + 1, k * 128:(k + 1) * 128]

    def pcat():
        return jnp.concatenate([pown[0:32, :], psib[0:32, :]], axis=1)

    def send_scores(index):
        done = {piece for group in GROUPS[:index + 1] for piece in group}
        before = {piece for group in GROUPS[:index] for piece in group}
        for slot in SLOTS:
            pieces = {slot + (0,), slot + (1,)}
            if not pieces <= done or pieces <= before:
                continue
            dx, d = slot
            target = ((1 - xh) if dx else xh) * 8 + (y - d + 8) % 8
            step = (target - layer + 16) % 16
            mate = xh * 16 + y * 2 + (1 - core)

            @pl.when(step == 0)
            def _():
                rx[0] = so[SLOT[slot], 0]

            @pl.when(step != 0)
            def _():
                remote(so.at[SLOT[slot], 0], rx.at[step * 2], fin_send, fin_recv, (target, block)).start()

            remote(so.at[SLOT[slot], 1], rx.at[step * 2 + 1], fin_send, fin_recv, (target, mate)).start()

    example = lax.broadcasted_iota(jnp.int32, (128, TOK), 0)
    onehot[0:128, 0:TOK] = (example == members).astype(F32).astype(BF16)
    onehot[0:128, TOK:] = jnp.zeros((128, TOK), BF16)
    onehot[128:, 0:TOK] = jnp.zeros((128, TOK), BF16)
    others = psib[32:48, :].astype(F32)[0:1, :]
    onehot[128:, TOK:] = (example.astype(F32) == others).astype(F32).astype(BF16)

    products(0)
    landed((0, 2, 0), (0, -2, 0), (1, 1, 0), (1, -1, 0), (0, 2, 1), (0, -2, 1), (1, 1, 1), (1, -1, 1))

    remote(pm.at[pl.ds(1, 7)], pm.at[pl.ds(1, 7)], msg_send.at[1], msg_recv.at[1], sibling).wait_recv()
    across = remote(pm, ps, msg_send.at[2], msg_recv.at[2], sibling)
    across.start()
    products(1)
    landed((0, 3, 0), (0, -3, 0))

    across.wait_recv()
    total = pm[0] + ps[0]
    for n in range(1, 8):
        total = total + (pm[n] + ps[n])
    moments = jnp.concatenate([total[:, 0:32], total[:, 64:96]], axis=0) * (1.0 / TOKENS)
    for i, (dx, d, p) in enumerate(ORDER):
        source = (ps if p else pm)[(d + 8) % 8]
        at = 32 + 16 * dx
        rall[0:8, 16 * i:16 * i + 16] = source[:, at:at + 16]
        rall[8:16, 16 * i:16 * i + 16] = source[:, at + 64:at + 80]
    diagonal = (
        lax.broadcasted_iota(jnp.int32, (RANK, RANK), 0) == lax.broadcasted_iota(jnp.int32, (RANK, RANK), 1)
    ).astype(F32)
    scales = []
    for i in (0, 1):
        part = moments[:, RANK * i:RANK * (i + 1)]
        trace = jnp.sum(jnp.sum(part * diagonal, axis=1, keepdims=True), axis=0, keepdims=True)
        scale = 1.0 / trace
        scales.append(scale)
        work[i] = jnp.concatenate([part * scale + (0.1 / RANK) * diagonal, diagonal], axis=1)

    def eliminate(begin, end):
        row = lax.broadcasted_iota(jnp.int32, (RANK, 2 * RANK), 0)
        tables = [work[0], work[1]]
        for k in range(begin, end):
            for i in (0, 1):
                table = tables[i]
                pivot = table[k:k + 1, :] / table[k:k + 1, k:k + 1]
                tables[i] = jnp.where(row == k, pivot, table - table[:, k:k + 1] * pivot)
        work[0] = tables[0]
        work[1] = tables[1]

    landed((0, 3, 1), (0, -3, 1))
    eliminate(0, 4)
    landed((1, 2, 0), (1, -2, 0))
    eliminate(4, 8)
    landed((1, 2, 1), (1, -2, 1))
    eliminate(8, 12)
    landed((1, 3, 0))
    eliminate(12, 16)
    landed((1, 3, 1))
    kind = lax.broadcasted_iota(jnp.int32, (RANK, 32 * ROWS), 1) % ROWS
    solved_grad = dot(work[0][:, RANK:], rall[...] * scales[0], NN, HIGHEST)
    solved_act = dot(work[1][:, RANK:], rall[...] * scales[1], NN, HIGHEST)
    solved = jnp.concatenate(
        [jnp.where(kind < 8, solved_grad, 0.0), jnp.where(kind < 8, 0.0, solved_act)], axis=0
    )
    vb[...] = solved.T.astype(BF16)
    pl.semaphore_wait(known.at[2], 1)
    products(2)
    for index in (0, 1, 2):
        scores(index)
        send_scores(index)
    landed((0, 4, 0), (0, 4, 1))
    products(3)
    scores(3)
    send_scores(3)
    landed((1, -3, 0), (1, -3, 1), (1, 4, 0), (1, 4, 1))
    products(4)
    scores(4)
    send_scores(4)

    tail = rx.at[pl.ds(1, 31)]
    remote(tail, tail, fin_send, fin_recv, sibling).wait()
    same, other = rx[0], rx[1]
    for i in range(1, 16):
        same = same + rx[2 * i]
        other = other + rx[2 * i + 1]
    first = same[0:1, 0:32] + other[1:2, 0:32]
    second = same[1:2, 0:32] + other[0:1, 0:32]
    scale = 1.0 / (8.0 * math.sqrt(2.0 * RANK * WIDTH * 16))
    out_ref[0:1, :] = jnp.where(core == 0, first, second) * scale
    out_ref[1:2, :] = jnp.where(core == 0, second, first) * scale

    sent = q.at[pl.ds(0, 30 * ROWS)]
    remote(sent, sent, send_sem, piece_sem.at[0], partner).wait_send()
    for copy in side:
        copy.wait_send()
    to_partner.wait_send()
    remote(pm.at[pl.ds(1, 7)], pm.at[pl.ds(1, 7)], msg_send.at[1], msg_recv.at[1], sibling).wait_send()
    across.wait_send()


def local(x, g, members, queries, down, up):
    hbm = pl.BlockSpec(memory_space=pltpu.HBM)
    vmem = pl.BlockSpec(memory_space=pltpu.VMEM)
    dma = pltpu.SemaphoreType.DMA
    out = pl.pallas_call(
        kernel,
        out_shape=jax.ShapeDtypeStruct((2, 32), F32),
        in_specs=[hbm] * 6,
        out_specs=vmem,
        scratch_shapes=[
            pltpu.VMEM((2 * TOK, HALF), BF16),
            pltpu.VMEM((2 * TOK, HALF), BF16),
            pltpu.VMEM((TOK, HALF), BF16),
            pltpu.VMEM((TOK, HALF), BF16),
            pltpu.VMEM((2 * RANK, HALF), BF16),
            pltpu.VMEM((2 * RANK, HALF), BF16),
            pltpu.VMEM((32 * ROWS, HALF), BF16),
            pltpu.VMEM((ROWS, HALF), BF16),
            pltpu.VMEM((8, 128), F32),
            pltpu.VMEM((8, 128), F32),
            pltpu.VMEM((8, 8, 128), F32),
            pltpu.VMEM((8, 8, 128), F32),
            pltpu.VMEM((48, TOK), BF16),
            pltpu.VMEM((48, TOK), BF16),
            pltpu.VMEM((2, RANK, 2 * RANK), F32),
            pltpu.VMEM((RANK, 32 * ROWS), F32),
            pltpu.VMEM((32 * ROWS, 2 * RANK), BF16),
            pltpu.VMEM((32 * ROWS, 2 * TOK), F32),
            pltpu.VMEM((256, 2 * TOK), BF16),
            pltpu.VMEM((16, 2, 8, 128), F32),
            pltpu.VMEM((32, 8, 128), F32),
            pltpu.VMEM((1, TOK), jnp.int32),
            dma((11,)),
            dma((32,)),
            dma,
            dma((4,)),
            dma((4,)),
            dma((3,)),
            dma((3,)),
            dma,
            dma,
            pltpu.SemaphoreType.REGULAR((3,)),
        ],
        compiler_params=pltpu.CompilerParams(
            collective_id=0, has_side_effects=True, vmem_limit_bytes=64 * 1024 * 1024
        ),
        name="influence",
    )(x, g, members, queries.reshape(ROWS, WIDTH), down, up)
    return out.T


def solution(mesh):
    placed = (
        P("layer", "dp", None),
        P("layer", "dp", None),
        P("dp", None),
        P("layer", "dp", None, None, None),
        P("layer", None, None),
        P("layer", None, None),
    )
    return jax.shard_map(
        local, mesh=mesh, in_specs=placed, out_specs=P("dp", "layer"), check_vma=False
    )
```

```python
import math

import jax
import jax.numpy as jnp
from jax import lax
from jax.experimental import pallas as pl
from jax.experimental.pallas import tpu as pltpu
from jax.sharding import PartitionSpec as P

MESH = pl.DeviceIdType.MESH
F32 = jnp.float32
BF16 = jnp.bfloat16
HIGHEST = lax.Precision.HIGHEST
NT = (((1,), (1,)), ((), ()))
NN = (((1,), (0,)), ((), ()))

TOK = 256
WIDTH = 4096
HALF = WIDTH // 2
RANK = 16
TOKENS = 8192
ROWS = 16

PARTS = 4
SPAN = HALF // PARTS
SLOTS = tuple((dx, d) for dx in (0, 1) for d in (0, 1, -1, 2, -2, 3, -3, 4))
SLOT = {slot: i for i, slot in enumerate(SLOTS)}

TREES = {
    (0, 0): "+-+-+-+xx-x-+-x",
    (0, 1): "+-+-+--xxxx-+x-",
    (0, 2): "+-+-+--xxxx-+--",
    (0, 3): "+-+-+-+xxxx-+x+",
    (1, 0): "+-+-+-+xxxxx+xx",
    (1, 1): "+-+-+-+xx-x-xxx",
    (1, 2): "+-+-+--xxx+xxx+",
    (1, 3): "+-+-+-+x+x+-x-x",
}

GROUPS = (
    ((0, 0, 0), (0, 0, 1), (0, 1, 0), (0, -1, 0), (1, 0, 0), (0, 1, 1), (0, -1, 1), (1, 0, 1),
     (0, 2, 0), (0, -2, 0), (1, 1, 0), (0, 2, 1)),
    ((1, -1, 0), (0, -2, 1), (1, 1, 1), (0, 3, 0), (1, -1, 1), (0, -3, 0), (0, 3, 1), (1, 2, 0),
     (1, -2, 0), (1, 2, 1), (0, -3, 1), (0, 4, 0), (1, -2, 1), (1, -3, 0)),
    ((0, 4, 1), (1, 3, 0), (1, 3, 1), (1, -3, 1), (1, 4, 1), (1, 4, 0)),
)
ORDER = tuple(query for group in GROUPS for query in group)
POS = {query: i for i, query in enumerate(ORDER)}

STEPS = (
    (0, 0, 0, 0), (0, 0, 0, 1), (0, 0, 0, 2), (0, 0, 0, 3), ("gproj",), (0, 0, 1, 0), (0, 0, 1, 1), (0, 0, 1, 2),
    (0, 0, 1, 3), ("aproj",), ("moments",), (0, 1, 0, 0), (0, -1, 0, 0), (0, 1, 0, 1), (0, -1, 0, 1), (1, 0, 0, 0),
    (0, 1, 0, 2), (0, -1, 0, 2), ("onehot",), (1, 0, 0, 1), (0, 1, 0, 3), (0, -1, 0, 3), (1, 0, 0, 2), (0, 1, 1, 0),
    (0, -1, 1, 0), (1, 0, 0, 3), (0, 1, 1, 1), (0, -1, 1, 1), (1, 0, 1, 0), (0, 1, 1, 2), (0, -1, 1, 2), (1, 0, 1, 1),
    (0, 1, 1, 3), (0, -1, 1, 3), (1, 0, 1, 2), (0, 2, 0, 0), (0, -2, 0, 0), ("pair",), (1, 0, 1, 3), (0, 2, 0, 1),
    (0, -2, 0, 1), (1, 1, 0, 0), (0, 2, 0, 2), (1, -1, 0, 0), (1, 1, 0, 1), (0, 2, 0, 3), (0, -2, 0, 2),
    (1, -1, 0, 1), (0, -2, 0, 3), (0, 2, 1, 0), (1, 1, 0, 2), (0, -2, 1, 0), (0, 2, 1, 1), ("sides",),
    ("products", 0, 0, "x"), (1, -1, 0, 2), (0, -2, 1, 1), (0, 2, 1, 2), (1, 1, 0, 3), ("products", 0, 0, "g"),
    (0, -2, 1, 2), (0, 2, 1, 3), (1, -1, 0, 3), (1, -1, 1, 1), ("products", 0, 1, "x"), (0, 3, 0, 0), (1, 1, 1, 0),
    (0, -2, 1, 3), (1, 1, 1, 3), (1, -1, 1, 0), ("products", 0, 1, "g"), (0, -3, 0, 0), (0, 3, 0, 1), (1, 1, 1, 1),
    (0, -3, 0, 1), (0, 3, 0, 2), (1, 1, 1, 2), (1, -2, 0, 0), (0, 3, 0, 3), (1, -1, 1, 2), (0, -3, 0, 2),
    (0, 3, 1, 0), (1, -1, 1, 3), (1, -2, 0, 1), (0, 3, 1, 1), (1, 2, 0, 0), (0, -3, 0, 3), (0, 3, 1, 2), (1, 2, 0, 1),
    (0, -3, 1, 0), ("across",), (0, 3, 1, 3), (1, 2, 0, 2), (1, -2, 0, 2), (1, 2, 0, 3), (0, 4, 0, 0), (0, -3, 1, 1),
    (1, 2, 1, 0), (1, 2, 1, 3), (0, -3, 1, 2), ("eliminate", 0), (1, -2, 1, 0), (1, -2, 0, 3), (1, 2, 1, 2),
    (1, 2, 1, 1), (1, -2, 1, 1), (0, 4, 0, 3), ("eliminate", 1), (1, -2, 1, 2), (0, -3, 1, 3), (0, 4, 1, 0),
    ("eliminate", 2), (1, -3, 0, 1), (0, 4, 0, 1), (0, 4, 1, 1), ("eliminate", 3), (1, -3, 0, 0), (1, 3, 0, 0),
    ("solve",), (1, 3, 1, 1), (0, 4, 0, 2), (1, 3, 0, 1), (1, -3, 0, 3), ("products", 1, 0, "x"), (1, -2, 1, 3),
    (0, 4, 1, 3), (1, 3, 1, 2), (1, -3, 0, 2), (1, 3, 0, 2), ("products", 1, 0, "g"), (1, -3, 1, 0), (0, 4, 1, 2),
    (1, 3, 0, 3), (1, 3, 1, 3), ("products", 1, 1, "x"), (1, 3, 1, 0), (1, 4, 0, 0), ("products", 1, 1, "g"),
    (1, -3, 1, 1), ("scores", 0), (1, -3, 1, 2), (1, 4, 0, 1), (1, 4, 1, 0), ("scores", 1), (1, 4, 1, 1),
    ("products", 2, 0, "x"), (1, -3, 1, 3), (1, 4, 1, 2), ("products", 2, 0, "g"), (1, 4, 0, 2), (1, 4, 0, 3),
    (1, 4, 1, 3), ("products", 2, 1, "x"), ("products", 2, 1, "g"), ("scores", 2),
)

def onward_table():
    table = {}
    for (p, h), links in TREES.items():
        for (dx, d), way in zip(SLOTS[1:], links):
            if way == "x":
                source = (1 - dx, d)
            elif way == "+":
                source = (dx, d - 1)
            else:
                source = (dx, -3 if d == 4 else d + 1)
            table.setdefault(source + (p, h), []).append((way, (dx, d, p, h)))
    return table


ONWARD = onward_table()


def dot(a, b, dims, precision=None):
    return lax.dot_general(a, b, dims, precision=precision, preferred_element_type=F32)


def kernel(
    x_ref, g_ref, member_ref, query_ref, down_ref, up_ref, out_ref,
    xb, gb, xo, go, fm, fo, q, qo, mine, theirs, pm, ps, pown, psib,
    work, rall, vb, kst, onehot, so, rx,
    mem, load_sem, piece_sem, send_sem, side_send, side_recv, msg_send, msg_recv, fin_send, fin_recv, known,
):
    layer, block = lax.axis_index("layer"), lax.axis_index("dp")
    xh, y, core = block // 16, (block // 2) % 8, block % 2
    z, xl = layer // 2, layer % 2

    def along_y(n):
        return (layer, xh * 16 + ((y + n + 8) % 8) * 2 + core)

    def along_z(n):
        return (((z + n + 8) % 8) * 2 + xl, block)

    partner = (layer, (1 - xh) * 16 + y * 2 + core)
    sibling = (layer, xh * 16 + y * 2 + (1 - core))
    beside = (z * 2 + (1 - xl), block)
    ways = {"+": along_y(1), "-": along_y(-1), "x": partner}

    def remote(src, dst, ssem, rsem, device):
        return pltpu.make_async_remote_copy(
            src_ref=src, dst_ref=dst, send_sem=ssem, recv_sem=rsem, device_id=device, device_id_type=MESH
        )

    def signal(sem, device):
        pl.semaphore_signal(sem, inc=1, device_id=device, device_id_type=MESH)

    def rows(piece):
        return pl.ds(POS[piece] * ROWS, ROWS)

    here = pl.ds(pl.multiple_of(core * HALF, HALF), HALF)
    there = pl.ds(pl.multiple_of((1 - core) * HALF, HALF), HALF)

    near = (
        along_y(1), along_y(-1), along_y(2), along_y(-2), partner, sibling,
        beside, along_z(1), along_z(-1), along_z(2), along_z(-2),
    )
    barrier = pltpu.get_barrier_semaphore()
    for device in near:
        signal(barrier, device)

    loads = [
        pltpu.make_async_copy(query_ref.at[:, here], q.at[rows((0, 0, 0))], load_sem.at[0]),
        pltpu.make_async_copy(query_ref.at[:, there], qo, load_sem.at[1]),
        pltpu.make_async_copy(up_ref.at[0, :, here], fm.at[pl.ds(0, RANK)], load_sem.at[2]),
        pltpu.make_async_copy(up_ref.at[0, :, there], fo.at[pl.ds(0, RANK)], load_sem.at[3]),
        pltpu.make_async_copy(down_ref.at[0, :, here], fm.at[pl.ds(RANK, RANK)], load_sem.at[4]),
        pltpu.make_async_copy(down_ref.at[0, :, there], fo.at[pl.ds(RANK, RANK)], load_sem.at[5]),
        pltpu.make_async_copy(g_ref.at[0, :, here], gb.at[pl.ds(0, TOK)], load_sem.at[6]),
        pltpu.make_async_copy(g_ref.at[0, :, there], go, load_sem.at[7]),
        pltpu.make_async_copy(x_ref.at[0, :, here], xb.at[pl.ds(0, TOK)], load_sem.at[8]),
        pltpu.make_async_copy(x_ref.at[0, :, there], xo, load_sem.at[9]),
        pltpu.make_async_copy(member_ref, mem, load_sem.at[10]),
    ]
    for copy in loads:
        copy.start()
    so[...] = jnp.zeros(so.shape, F32)
    loads[0].wait()
    loads[1].wait()

    pl.semaphore_wait(barrier, len(near))

    def part(query, h):
        return q.at[rows(query), pl.ds(h * SPAN, SPAN)]

    def onward(piece):
        for way, there_piece in ONWARD.get(piece, ()):
            query, h = there_piece[:3], there_piece[3]
            remote(
                part(piece[:3], h), part(query, h), send_sem, piece_sem.at[POS[query], h], ways[way]
            ).start()

    def landed(piece):
        query, h = piece[:3], piece[3]
        if query == (0, 0, 1):
            side[h].wait_recv()
        elif query != (0, 0, 0):
            remote(part(query, h), part(query, h), send_sem, piece_sem.at[POS[query], h], partner).wait_recv()
        onward(piece)

    side = [
        remote(
            qo.at[:, pl.ds(h * SPAN, SPAN)], part((0, 0, 1), h), side_send.at[h], piece_sem.at[POS[(0, 0, 1)], h], sibling
        )
        for h in range(PARTS)
    ]
    rest = [
        remote(go, gb.at[pl.ds(TOK, TOK)], side_send.at[PARTS], side_recv.at[0], sibling),
        remote(xo, xb.at[pl.ds(TOK, TOK)], side_send.at[PARTS + 1], side_recv.at[1], sibling),
        remote(pown, psib, side_send.at[PARTS + 2], side_recv.at[2], sibling),
    ]
    to_partner = remote(mine, theirs, msg_send.at[0], msg_recv.at[0], partner)
    pair = [remote(pm.at[0], pm.at[n], msg_send.at[1], msg_recv.at[1], along_y(n)) for n in range(1, 8)]
    pairs = remote(pm.at[pl.ds(1, 7)], pm.at[pl.ds(1, 7)], msg_send.at[1], msg_recv.at[1], sibling)
    across = remote(pm, ps, msg_send.at[2], msg_recv.at[2], sibling)

    def step_gproj():
        for copy in loads[2:8]:
            copy.wait()
        rest[0].start()
        projections["own"] = dot(fm[...], q[rows((0, 0, 0)), :], NT) + dot(fo[...], qo[...], NT)
        projections["grad"] = dot(fm[0:RANK, :], gb[0:TOK, :], NT) + dot(fo[0:RANK, :], go[...], NT)

    def step_aproj():
        loads[8].wait()
        loads[9].wait()
        rest[1].start()
        projections["act"] = dot(fm[RANK:, :], xb[0:TOK, :], NT) + dot(fo[RANK:, :], xo[...], NT)

    def step_moments():
        own_q = projections["own"]
        query_proj = jnp.concatenate([own_q[0:RANK, 8:16], own_q[RANK:, 0:8]], axis=1)
        proj = jnp.concatenate([projections["grad"], projections["act"]], axis=0)
        cov = dot(proj, proj, NT, HIGHEST)
        both = jnp.concatenate(
            [cov[0:RANK, 0:RANK], cov[RANK:, RANK:], query_proj, jnp.zeros((RANK, 16), F32)], axis=1
        )
        mine[...] = jnp.concatenate([both[0:8], both[8:16]], axis=1)
        to_partner.start()
        loads[10].wait()
        pown[0:32, :] = proj.astype(BF16)
        pown[32:48, :] = jnp.broadcast_to(mem[...].astype(F32), (16, TOK)).astype(BF16)
        rest[2].start()

    def step_pair():
        pl.semaphore_wait(known.at[0], 4)
        signal(known.at[1], beside)
        to_partner.wait_recv()
        lane = lax.broadcasted_iota(jnp.int32, (8, 128), 1) % 64
        from_x = theirs[...]
        own = mine[...]
        pm[0] = jnp.where(lane < 32, own + from_x, jnp.where(lane < 48, own, pltpu.roll(from_x, 16, 1)))
        for copy in pair:
            copy.start()

    def step_across():
        pl.semaphore_wait(known.at[1], 1)
        signal(known.at[2], sibling)
        pairs.wait_recv()
        across.start()

    def step_onehot():
        rest[2].wait_recv()
        example = lax.broadcasted_iota(jnp.int32, (128, TOK), 0)
        onehot[0:128, 0:TOK] = (example == mem[...]).astype(F32).astype(BF16)
        onehot[0:128, TOK:] = jnp.zeros((128, TOK), BF16)
        onehot[128:, 0:TOK] = jnp.zeros((128, TOK), BF16)
        others = psib[32:48, :].astype(F32)[0:1, :]
        onehot[128:, TOK:] = (example.astype(F32) == others).astype(F32).astype(BF16)

    def step_sides():
        rest[0].wait_recv()
        rest[1].wait_recv()

    def span(index):
        first = POS[GROUPS[index][0]] * ROWS
        return first, len(GROUPS[index]) * ROWS

    def step_products(index, h, operand):
        first, count = span(index)
        columns = slice(h * (HALF // 2), (h + 1) * (HALF // 2))
        rows_of, lift = (xb, 0) if operand == "x" else (gb, 8)
        found = dot(q[first:first + count, columns], rows_of[:, columns], NT)
        for i in range(lift, count, ROWS):
            if h == 0:
                kst[first + i:first + i + 8, :] = found[i:i + 8]
            else:
                kst[first + i:first + i + 8, :] += found[i:i + 8]

    def step_eliminate(quarter):
        if quarter == 0:
            across.wait_recv()
            total = pm[0] + ps[0]
            for n in range(1, 8):
                total = total + (pm[n] + ps[n])
            moments = jnp.concatenate([total[:, 0:32], total[:, 64:96]], axis=0) * (1.0 / TOKENS)
            for i, (dx, d, p) in enumerate(ORDER):
                source = (ps if p else pm)[(d + 8) % 8]
                at = 32 + 16 * dx
                rall[0:8, 16 * i:16 * i + 16] = source[:, at:at + 16]
                rall[8:16, 16 * i:16 * i + 16] = source[:, at + 64:at + 80]
            diagonal = (
                lax.broadcasted_iota(jnp.int32, (RANK, RANK), 0) == lax.broadcasted_iota(jnp.int32, (RANK, RANK), 1)
            ).astype(F32)
            for i in (0, 1):
                moment = moments[:, RANK * i:RANK * (i + 1)]
                trace = jnp.sum(jnp.sum(moment * diagonal, axis=1, keepdims=True), axis=0, keepdims=True)
                scales.append(1.0 / trace)
                work[i] = jnp.concatenate([moment * scales[i] + (0.1 / RANK) * diagonal, diagonal], axis=1)
        row = lax.broadcasted_iota(jnp.int32, (RANK, 2 * RANK), 0)
        tables = [work[0], work[1]]
        for k in range(4 * quarter, 4 * quarter + 4):
            for i in (0, 1):
                table = tables[i]
                pivot = table[k:k + 1, :] / table[k:k + 1, k:k + 1]
                tables[i] = jnp.where(row == k, pivot, table - table[:, k:k + 1] * pivot)
        work[0] = tables[0]
        work[1] = tables[1]

    def step_solve():
        kind = lax.broadcasted_iota(jnp.int32, (RANK, 32 * ROWS), 1) % ROWS
        solved_grad = dot(work[0][:, RANK:], rall[...] * scales[0], NN, HIGHEST)
        solved_act = dot(work[1][:, RANK:], rall[...] * scales[1], NN, HIGHEST)
        solved = jnp.concatenate(
            [jnp.where(kind < 8, solved_grad, 0.0), jnp.where(kind < 8, 0.0, solved_act)], axis=0
        )
        vb[...] = solved.T.astype(BF16)
        pl.semaphore_wait(known.at[2], 1)

    def step_scores(index):
        first, count = span(index)
        group = GROUPS[index]
        both_proj = jnp.concatenate([pown[0:32, :], psib[0:32, :]], axis=1)
        weights = dot(vb[first:first + count, :], both_proj, NN)
        terms = (weights * kst[first:first + count, :]).reshape(len(group), ROWS, 2 * TOK)
        terms = jnp.sum(terms, axis=1)
        high = terms.astype(BF16)
        low = (terms - high.astype(F32)).astype(BF16)
        sums = dot(high, onehot[...], NT) + dot(low, onehot[...], NT)
        for i, (dx, d, p) in enumerate(group):
            for k in (0, 1):
                so[SLOT[dx, d], k, p:p + 1, :] = sums[i:i + 1, k * 128:(k + 1) * 128]
        done = {query for members in GROUPS[:index + 1] for query in members}
        before = {query for members in GROUPS[:index] for query in members}
        mate = xh * 16 + y * 2 + (1 - core)
        for slot in SLOTS:
            queries = {slot + (0,), slot + (1,)}
            if not queries <= done or queries <= before:
                continue
            dx, d = slot
            target = ((1 - xh) if dx else xh) * 8 + (y - d + 8) % 8
            step = (target - layer + 16) % 16

            @pl.when(step == 0)
            def _():
                rx[0] = so[SLOT[slot], 0]

            @pl.when(step != 0)
            def _():
                remote(so.at[SLOT[slot], 0], rx.at[step * 2], fin_send, fin_recv, (target, block)).start()

            remote(so.at[SLOT[slot], 1], rx.at[step * 2 + 1], fin_send, fin_recv, (target, mate)).start()

    projections, scales = {}, []
    work_of = {
        "gproj": step_gproj, "aproj": step_aproj, "moments": step_moments, "pair": step_pair,
        "across": step_across, "onehot": step_onehot, "sides": step_sides, "products": step_products,
        "eliminate": step_eliminate, "solve": step_solve, "scores": step_scores,
    }
    started = False
    for item in STEPS:
        if isinstance(item[0], str):
            work_of[item[0]](*item[1:])
            continue
        landed(item)
        if not started and item[:3] == (0, 0, 0) and item[3] == PARTS - 1:
            started = True
            for copy in side:
                copy.start()
            for device in (along_y(2), along_y(-2), along_z(2), along_z(-2)):
                signal(known.at[0], device)

    tail = rx.at[pl.ds(1, 31)]
    remote(tail, tail, fin_send, fin_recv, sibling).wait()
    same, other = rx[0], rx[1]
    for i in range(1, 16):
        same = same + rx[2 * i]
        other = other + rx[2 * i + 1]
    first = same[0:1, 0:32] + other[1:2, 0:32]
    second = same[1:2, 0:32] + other[0:1, 0:32]
    scale = 1.0 / (8.0 * math.sqrt(2.0 * RANK * WIDTH * 16))
    out_ref[0:1, :] = jnp.where(core == 0, first, second) * scale
    out_ref[1:2, :] = jnp.where(core == 0, second, first) * scale

    sent = q.at[pl.ds(0, 30 * ROWS)]
    remote(sent, sent, send_sem, piece_sem.at[0, 0], partner).wait_send()
    for copy in side + rest:
        copy.wait_send()
    to_partner.wait_send()
    pairs.wait_send()
    across.wait_send()


def local(x, g, members, queries, down, up):
    hbm = pl.BlockSpec(memory_space=pltpu.HBM)
    vmem = pl.BlockSpec(memory_space=pltpu.VMEM)
    dma = pltpu.SemaphoreType.DMA
    out = pl.pallas_call(
        kernel,
        out_shape=jax.ShapeDtypeStruct((2, 32), F32),
        in_specs=[hbm] * 6,
        out_specs=vmem,
        scratch_shapes=[
            pltpu.VMEM((2 * TOK, HALF), BF16),
            pltpu.VMEM((2 * TOK, HALF), BF16),
            pltpu.VMEM((TOK, HALF), BF16),
            pltpu.VMEM((TOK, HALF), BF16),
            pltpu.VMEM((2 * RANK, HALF), BF16),
            pltpu.VMEM((2 * RANK, HALF), BF16),
            pltpu.VMEM((32 * ROWS, HALF), BF16),
            pltpu.VMEM((ROWS, HALF), BF16),
            pltpu.VMEM((8, 128), F32),
            pltpu.VMEM((8, 128), F32),
            pltpu.VMEM((8, 8, 128), F32),
            pltpu.VMEM((8, 8, 128), F32),
            pltpu.VMEM((48, TOK), BF16),
            pltpu.VMEM((48, TOK), BF16),
            pltpu.VMEM((2, RANK, 2 * RANK), F32),
            pltpu.VMEM((RANK, 32 * ROWS), F32),
            pltpu.VMEM((32 * ROWS, 2 * RANK), BF16),
            pltpu.VMEM((32 * ROWS, 2 * TOK), F32),
            pltpu.VMEM((256, 2 * TOK), BF16),
            pltpu.VMEM((16, 2, 8, 128), F32),
            pltpu.VMEM((32, 8, 128), F32),
            pltpu.VMEM((1, TOK), jnp.int32),
            dma((11,)),
            dma((32, PARTS)),
            dma,
            dma((PARTS + 3,)),
            dma((3,)),
            dma((3,)),
            dma((3,)),
            dma,
            dma,
            pltpu.SemaphoreType.REGULAR((3,)),
        ],
        compiler_params=pltpu.CompilerParams(
            collective_id=0, has_side_effects=True, vmem_limit_bytes=64 * 1024 * 1024
        ),
        name="influence",
    )(x, g, members, queries.reshape(ROWS, WIDTH), down, up)
    return out.T


def solution(mesh):
    placed = (
        P("layer", "dp", None),
        P("layer", "dp", None),
        P("dp", None),
        P("layer", "dp", None, None, None),
        P("layer", None, None),
        P("layer", None, None),
    )
    return jax.shard_map(
        local, mesh=mesh, in_specs=placed, out_specs=P("dp", "layer"), check_vma=False
    )
```

```python
import math

import jax
import jax.numpy as jnp
from jax import lax
from jax.experimental import pallas as pl
from jax.experimental.pallas import tpu as pltpu
from jax.sharding import PartitionSpec as P

MESH = pl.DeviceIdType.MESH
F32 = jnp.float32
BF16 = jnp.bfloat16
HIGHEST = lax.Precision.HIGHEST
NT = (((1,), (1,)), ((), ()))
NN = (((1,), (0,)), ((), ()))

TOK = 256
WIDTH = 4096
HALF = WIDTH // 2
RANK = 16
TOKENS = 8192
ROWS = 16

PARTS = 2
SPAN = HALF // PARTS
SLOTS = tuple((dx, d) for dx in (0, 1) for d in (0, 1, -1, 2, -2, 3, -3, 4))
SLOT = {slot: i for i, slot in enumerate(SLOTS)}

GROUPS = (
    ((0, 0, 0), (0, 0, 1), (0, 1, 0), (0, -1, 0), (1, 0, 0), (0, 1, 1), (0, -1, 1), (1, 0, 1),
     (0, 2, 0), (0, -2, 0), (1, -1, 0), (0, 2, 1), (0, -2, 1), (1, 1, 0), (1, -1, 1), (0, -3, 0),
     (1, 1, 1), (0, 3, 0), (0, -3, 1), (1, 2, 1), (1, 2, 0), (1, -2, 0), (0, 3, 1), (1, -2, 1)),
    ((0, 4, 0), (0, 4, 1), (1, -3, 1), (1, 3, 1), (1, -3, 0), (1, 3, 0), (1, 4, 0), (1, 4, 1)),
)
ORDER = tuple(query for group in GROUPS for query in group)
POS = {query: i for i, query in enumerate(ORDER)}

STEPS = (
    (0, 0, 0, 0), (0, 0, 0, 0, "+"), (0, 0, 0, 0, "-"), (0, 0, 0, 1), (0, 0, 0, 0, "x"), (0, 0, 0, 1, "+"),
    (0, 0, 0, 1, "x"), (0, 0, 0, 1, "-"), (0, 0, 1, 0), (0, 0, 1, 1), (0, 0, 1, 1, "x"), (0, 0, 1, 0, "-"),
    (0, 0, 1, 1, "+"), ("gproj",), (0, 0, 1, 0, "+"), (0, 0, 1, 1, "-"), ("aproj",), ("moments",), ("known",),
    (0, 0, 1, 0, "x"), (0, 1, 0, 0), (0, -1, 0, 0), (0, -1, 0, 0, "-"), (0, -1, 0, 0, "x"), (0, 1, 0, 0, "+"),
    (1, 0, 0, 0), (0, -1, 0, 1), (0, -1, 0, 1, "-"), (1, 0, 0, 0, "+"), (0, -1, 0, 1, "x"), (0, 1, 0, 1),
    (0, 1, 0, 1, "x"), (0, 1, 1, 1), (0, -1, 1, 0), (0, -1, 1, 0, "-"), (0, 1, 1, 1, "+"), (0, -1, 1, 1),
    (1, 0, 0, 1), (0, 1, 1, 0), (0, 1, 0, 1, "+"), (1, 0, 1, 1), (0, 1, 1, 0, "+"), (1, 0, 1, 1, "+"),
    (0, -1, 1, 1, "x"), (0, -1, 1, 1, "-"), (0, -2, 0, 0), (0, -2, 0, 0, "-"), (0, 2, 0, 0), ("sides",),
    (0, 1, 1, 0, "x"), ("pair",), (0, 2, 0, 0, "+"), (0, -1, 1, 0, "x"), (0, -2, 0, 1), (0, -2, 0, 1, "-"),
    (0, -2, 1, 0), (0, -2, 1, 0, "-"), (0, 2, 1, 1), (0, 2, 1, 1, "x"), (1, -1, 0, 0), (1, -1, 0, 0, "-"),
    (1, 1, 0, 0), (1, 1, 0, 0, "+"), ("onehot",), (0, -2, 1, 0, "x"), (0, 2, 0, 1), (0, -2, 1, 1), (0, -2, 1, 1, "-"),
    (0, 2, 0, 1, "+"), (0, 2, 1, 0), (0, 2, 1, 0, "x"), (0, 2, 1, 0, "+"), (0, 2, 1, 1, "+"), (0, -3, 0, 0),
    (0, -3, 0, 0, "-"), (1, -1, 1, 1), (0, -3, 0, 1), (0, -3, 0, 1, "x"), (1, 1, 0, 1), (1, -1, 0, 1), (1, 0, 1, 0),
    (1, -1, 1, 1, "-"), (1, 1, 0, 1, "+"), (1, -1, 0, 1, "-"), (0, -3, 0, 1, "-"), (0, -3, 1, 0), (0, -3, 1, 0, "x"),
    (1, -1, 1, 0), (1, 1, 1, 0), (1, 2, 1, 1), (1, 2, 1, 1, "+"), (0, 3, 0, 0), (1, -2, 0, 0), (0, 3, 0, 1),
    (0, 3, 0, 1, "x"), (1, -2, 0, 0, "-"), (0, -3, 1, 1), (0, -3, 1, 1, "x"), (1, 2, 0, 0), (1, 2, 0, 0, "+"),
    (1, 2, 1, 0), (0, 3, 1, 0), ("across",), (0, -3, 1, 1, "-"), (0, 4, 0, 0), (1, -2, 1, 0), (0, 4, 0, 0, "x"),
    (0, 3, 1, 0, "+"), ("products", 0, 0, 1, "g"), ("products", 0, 0, 1, "x"), (1, 2, 1, 0, "+"), (1, -3, 0, 1),
    (1, -3, 0, 1, "-"), ("eliminate", 0), (0, 3, 1, 1), (1, 1, 1, 1), (1, -2, 0, 1), (1, -2, 1, 1), (1, 2, 0, 1),
    (1, -3, 1, 0), (1, -3, 1, 0, "-"), (1, 3, 1, 1), (1, 3, 1, 1, "+"), ("eliminate", 1), ("products", 0, 1, 2, "x"),
    ("products", 0, 1, 2, "g"), ("eliminate", 2), ("eliminate", 3), (0, 4, 1, 0), (1, -3, 0, 0), (0, 4, 1, 1),
    (1, 3, 0, 1), ("solve",), (1, 3, 0, 0), ("scores", 0), (1, 4, 1, 0), (0, 4, 0, 1), (1, 3, 1, 0), (1, 4, 0, 0),
    ("products", 1, 0, 1, "x"), (1, 4, 0, 1), (1, 4, 1, 1), (1, -3, 1, 1), ("products", 1, 0, 1, "g"),
    ("products", 1, 1, 2, "x"), ("products", 1, 1, 2, "g"), ("scores", 1),
)

def moved(query, way):
    dx, d, p = query
    if way == "x":
        return (1 - dx, d, p)
    d = d + 1 if way == "+" else d - 1
    return (dx, 4 if d == -4 else d, p)


def dot(a, b, dims, precision=None):
    return lax.dot_general(a, b, dims, precision=precision, preferred_element_type=F32)


def kernel(
    x_ref, g_ref, member_ref, query_ref, down_ref, up_ref, out_ref,
    xb, gb, xo, go, fm, fo, q, qo, mine, theirs, pm, ps, pown, psib,
    work, rall, vb, kst, onehot, so, rx,
    mem, load_sem, piece_sem, send_sem, side_send, side_recv, msg_send, msg_recv, fin_send, fin_recv, known,
):
    layer, block = lax.axis_index("layer"), lax.axis_index("dp")
    xh, y, core = block // 16, (block // 2) % 8, block % 2
    z, xl = layer // 2, layer % 2

    def along_y(n):
        return (layer, xh * 16 + ((y + n + 8) % 8) * 2 + core)

    def along_z(n):
        return (((z + n + 8) % 8) * 2 + xl, block)

    partner = (layer, (1 - xh) * 16 + y * 2 + core)
    sibling = (layer, xh * 16 + y * 2 + (1 - core))
    beside = (z * 2 + (1 - xl), block)
    ways = {"+": along_y(1), "-": along_y(-1), "x": partner}

    def remote(src, dst, ssem, rsem, device):
        return pltpu.make_async_remote_copy(
            src_ref=src, dst_ref=dst, send_sem=ssem, recv_sem=rsem, device_id=device, device_id_type=MESH
        )

    def signal(sem, device):
        pl.semaphore_signal(sem, inc=1, device_id=device, device_id_type=MESH)

    def rows(piece):
        return pl.ds(POS[piece] * ROWS, ROWS)

    here = pl.ds(pl.multiple_of(core * HALF, HALF), HALF)
    there = pl.ds(pl.multiple_of((1 - core) * HALF, HALF), HALF)

    near = (
        along_y(1), along_y(-1), partner, sibling, beside, along_z(1), along_z(-1),
    )
    barrier = pltpu.get_barrier_semaphore()
    for device in near:
        signal(barrier, device)

    loads = [
        pltpu.make_async_copy(query_ref.at[:, here], q.at[rows((0, 0, 0))], load_sem.at[0]),
        pltpu.make_async_copy(query_ref.at[:, there], qo, load_sem.at[1]),
        pltpu.make_async_copy(up_ref.at[0, :, here], fm.at[pl.ds(0, RANK)], load_sem.at[2]),
        pltpu.make_async_copy(up_ref.at[0, :, there], fo.at[pl.ds(0, RANK)], load_sem.at[3]),
        pltpu.make_async_copy(down_ref.at[0, :, here], fm.at[pl.ds(RANK, RANK)], load_sem.at[4]),
        pltpu.make_async_copy(down_ref.at[0, :, there], fo.at[pl.ds(RANK, RANK)], load_sem.at[5]),
        pltpu.make_async_copy(g_ref.at[0, :, here], gb.at[pl.ds(0, TOK)], load_sem.at[6]),
        pltpu.make_async_copy(g_ref.at[0, :, there], go, load_sem.at[7]),
        pltpu.make_async_copy(x_ref.at[0, :, here], xb.at[pl.ds(0, TOK)], load_sem.at[8]),
        pltpu.make_async_copy(x_ref.at[0, :, there], xo, load_sem.at[9]),
        pltpu.make_async_copy(member_ref, mem, load_sem.at[10]),
    ]
    for copy in loads:
        copy.start()
    so[...] = jnp.zeros(so.shape, F32)
    loads[0].wait()
    loads[1].wait()

    pl.semaphore_wait(barrier, len(near))

    def part(query, h):
        return q.at[rows(query), pl.ds(h * SPAN, SPAN)]

    def passed_on(query, h, way):
        target = moved(query, way)
        remote(
            part(query, h), part(target, h), send_sem, piece_sem.at[POS[target], h], ways[way]
        ).start()

    def landed(query, h):
        if query == (0, 0, 1):
            side[h].wait_recv()
        elif query != (0, 0, 0):
            remote(part(query, h), part(query, h), send_sem, piece_sem.at[POS[query], h], partner).wait_recv()

    side = [
        remote(
            qo.at[:, pl.ds(h * SPAN, SPAN)], part((0, 0, 1), h), side_send.at[h], piece_sem.at[POS[(0, 0, 1)], h], sibling
        )
        for h in range(PARTS)
    ]
    rest = [
        remote(go, gb.at[pl.ds(TOK, TOK)], side_send.at[PARTS], side_recv.at[0], sibling),
        remote(xo, xb.at[pl.ds(TOK, TOK)], side_send.at[PARTS + 1], side_recv.at[1], sibling),
        remote(pown, psib, side_send.at[PARTS + 2], side_recv.at[2], sibling),
    ]
    to_partner = remote(mine, theirs, msg_send.at[0], msg_recv.at[0], partner)
    pair = [remote(pm.at[0], pm.at[n], msg_send.at[1], msg_recv.at[1], along_y(n)) for n in range(1, 8)]
    pairs = remote(pm.at[pl.ds(1, 7)], pm.at[pl.ds(1, 7)], msg_send.at[1], msg_recv.at[1], sibling)
    across = remote(pm, ps, msg_send.at[2], msg_recv.at[2], sibling)

    def step_gproj():
        for copy in loads[2:8]:
            copy.wait()
        rest[0].start()
        projections["own"] = dot(fm[...], q[rows((0, 0, 0)), :], NT) + dot(fo[...], qo[...], NT)
        projections["grad"] = dot(fm[0:RANK, :], gb[0:TOK, :], NT) + dot(fo[0:RANK, :], go[...], NT)

    def step_aproj():
        loads[8].wait()
        loads[9].wait()
        rest[1].start()
        projections["act"] = dot(fm[RANK:, :], xb[0:TOK, :], NT) + dot(fo[RANK:, :], xo[...], NT)

    def step_moments():
        own_q = projections["own"]
        query_proj = jnp.concatenate([own_q[0:RANK, 8:16], own_q[RANK:, 0:8]], axis=1)
        proj = jnp.concatenate([projections["grad"], projections["act"]], axis=0)
        cov = dot(proj, proj, NT, HIGHEST)
        both = jnp.concatenate(
            [cov[0:RANK, 0:RANK], cov[RANK:, RANK:], query_proj, jnp.zeros((RANK, 16), F32)], axis=1
        )
        mine[...] = jnp.concatenate([both[0:8], both[8:16]], axis=1)
        to_partner.start()
        loads[10].wait()
        pown[0:32, :] = proj.astype(BF16)
        pown[32:48, :] = jnp.broadcast_to(mem[...].astype(F32), (16, TOK)).astype(BF16)
        rest[2].start()

    def step_known():
        pl.semaphore_wait(known.at[0], 4)
        for device in (along_y(2), along_y(-2), along_z(2), along_z(-2)):
            signal(known.at[1], device)

    def step_pair():
        pl.semaphore_wait(known.at[1], 4)
        signal(known.at[2], beside)
        to_partner.wait_recv()
        lane = lax.broadcasted_iota(jnp.int32, (8, 128), 1) % 64
        from_x = theirs[...]
        own = mine[...]
        pm[0] = jnp.where(lane < 32, own + from_x, jnp.where(lane < 48, own, pltpu.roll(from_x, 16, 1)))
        for copy in pair:
            copy.start()

    def step_across():
        pl.semaphore_wait(known.at[2], 1)
        signal(known.at[3], sibling)
        pairs.wait_recv()
        across.start()

    def step_onehot():
        rest[2].wait_recv()
        example = lax.broadcasted_iota(jnp.int32, (128, TOK), 0)
        onehot[0:128, 0:TOK] = (example == mem[...]).astype(F32).astype(BF16)
        onehot[0:128, TOK:] = jnp.zeros((128, TOK), BF16)
        onehot[128:, 0:TOK] = jnp.zeros((128, TOK), BF16)
        others = psib[32:48, :].astype(F32)[0:1, :]
        onehot[128:, TOK:] = (example.astype(F32) == others).astype(F32).astype(BF16)

    def step_sides():
        rest[0].wait_recv()
        rest[1].wait_recv()

    def span(index):
        first = POS[GROUPS[index][0]] * ROWS
        return first, len(GROUPS[index]) * ROWS

    def step_products(index, begin, end, operand):
        first, count = span(index)
        columns = slice(begin * SPAN, end * SPAN)
        rows_of, lift = (xb, 0) if operand == "x" else (gb, 8)
        found = dot(q[first:first + count, columns], rows_of[:, columns], NT)
        for i in range(lift, count, ROWS):
            if begin == 0:
                kst[first + i:first + i + 8, :] = found[i:i + 8]
            else:
                kst[first + i:first + i + 8, :] += found[i:i + 8]

    def step_eliminate(quarter):
        if quarter == 0:
            across.wait_recv()
            total = pm[0] + ps[0]
            for n in range(1, 8):
                total = total + (pm[n] + ps[n])
            moments = jnp.concatenate([total[:, 0:32], total[:, 64:96]], axis=0) * (1.0 / TOKENS)
            for i, (dx, d, p) in enumerate(ORDER):
                source = (ps if p else pm)[(d + 8) % 8]
                at = 32 + 16 * dx
                rall[0:8, 16 * i:16 * i + 16] = source[:, at:at + 16]
                rall[8:16, 16 * i:16 * i + 16] = source[:, at + 64:at + 80]
            diagonal = (
                lax.broadcasted_iota(jnp.int32, (RANK, RANK), 0) == lax.broadcasted_iota(jnp.int32, (RANK, RANK), 1)
            ).astype(F32)
            for i in (0, 1):
                moment = moments[:, RANK * i:RANK * (i + 1)]
                trace = jnp.sum(jnp.sum(moment * diagonal, axis=1, keepdims=True), axis=0, keepdims=True)
                scales.append(1.0 / trace)
                work[i] = jnp.concatenate([moment * scales[i] + (0.1 / RANK) * diagonal, diagonal], axis=1)
        row = lax.broadcasted_iota(jnp.int32, (RANK, 2 * RANK), 0)
        tables = [work[0], work[1]]
        for k in range(4 * quarter, 4 * quarter + 4):
            for i in (0, 1):
                table = tables[i]
                pivot = table[k:k + 1, :] / table[k:k + 1, k:k + 1]
                tables[i] = jnp.where(row == k, pivot, table - table[:, k:k + 1] * pivot)
        work[0] = tables[0]
        work[1] = tables[1]

    def step_solve():
        kind = lax.broadcasted_iota(jnp.int32, (RANK, 32 * ROWS), 1) % ROWS
        solved_grad = dot(work[0][:, RANK:], rall[...] * scales[0], NN, HIGHEST)
        solved_act = dot(work[1][:, RANK:], rall[...] * scales[1], NN, HIGHEST)
        solved = jnp.concatenate(
            [jnp.where(kind < 8, solved_grad, 0.0), jnp.where(kind < 8, 0.0, solved_act)], axis=0
        )
        vb[...] = solved.T.astype(BF16)
        pl.semaphore_wait(known.at[3], 1)

    def step_scores(index):
        first, count = span(index)
        group = GROUPS[index]
        both_proj = jnp.concatenate([pown[0:32, :], psib[0:32, :]], axis=1)
        weights = dot(vb[first:first + count, :], both_proj, NN)
        terms = (weights * kst[first:first + count, :]).reshape(len(group), ROWS, 2 * TOK)
        terms = jnp.sum(terms, axis=1)
        high = terms.astype(BF16)
        low = (terms - high.astype(F32)).astype(BF16)
        sums = dot(high, onehot[...], NT) + dot(low, onehot[...], NT)
        for i, (dx, d, p) in enumerate(group):
            for k in (0, 1):
                so[SLOT[dx, d], k, p:p + 1, :] = sums[i:i + 1, k * 128:(k + 1) * 128]
        done = {query for members in GROUPS[:index + 1] for query in members}
        before = {query for members in GROUPS[:index] for query in members}
        mate = xh * 16 + y * 2 + (1 - core)
        for slot in SLOTS:
            queries = {slot + (0,), slot + (1,)}
            if not queries <= done or queries <= before:
                continue
            dx, d = slot
            target = ((1 - xh) if dx else xh) * 8 + (y - d + 8) % 8
            step = (target - layer + 16) % 16

            @pl.when(step == 0)
            def _():
                rx[0] = so[SLOT[slot], 0]

            @pl.when(step != 0)
            def _():
                remote(so.at[SLOT[slot], 0], rx.at[step * 2], fin_send, fin_recv, (target, block)).start()

            remote(so.at[SLOT[slot], 1], rx.at[step * 2 + 1], fin_send, fin_recv, (target, mate)).start()

    projections, scales = {}, []
    work_of = {
        "gproj": step_gproj, "aproj": step_aproj, "moments": step_moments, "known": step_known, "pair": step_pair,
        "across": step_across, "onehot": step_onehot, "sides": step_sides, "products": step_products,
        "eliminate": step_eliminate, "solve": step_solve, "scores": step_scores,
    }
    for copy in side:
        copy.start()
    for device in (along_y(1), along_y(-1), along_z(1), along_z(-1)):
        signal(known.at[0], device)
    for item in STEPS:
        if isinstance(item[0], str):
            work_of[item[0]](*item[1:])
        elif len(item) == 4:
            landed(item[:3], item[3])
        else:
            passed_on(item[:3], item[3], item[4])

    tail = rx.at[pl.ds(1, 31)]
    remote(tail, tail, fin_send, fin_recv, sibling).wait()
    same, other = rx[0], rx[1]
    for i in range(1, 16):
        same = same + rx[2 * i]
        other = other + rx[2 * i + 1]
    first = same[0:1, 0:32] + other[1:2, 0:32]
    second = same[1:2, 0:32] + other[0:1, 0:32]
    scale = 1.0 / (8.0 * math.sqrt(2.0 * RANK * WIDTH * 16))
    out_ref[0:1, :] = jnp.where(core == 0, first, second) * scale
    out_ref[1:2, :] = jnp.where(core == 0, second, first) * scale

    sent = q.at[pl.ds(0, 30 * ROWS)]
    remote(sent, sent, send_sem, piece_sem.at[0, 0], partner).wait_send()
    for copy in side + rest:
        copy.wait_send()
    to_partner.wait_send()
    pairs.wait_send()
    across.wait_send()


def local(x, g, members, queries, down, up):
    hbm = pl.BlockSpec(memory_space=pltpu.HBM)
    vmem = pl.BlockSpec(memory_space=pltpu.VMEM)
    dma = pltpu.SemaphoreType.DMA
    out = pl.pallas_call(
        kernel,
        out_shape=jax.ShapeDtypeStruct((2, 32), F32),
        in_specs=[hbm] * 6,
        out_specs=vmem,
        scratch_shapes=[
            pltpu.VMEM((2 * TOK, HALF), BF16),
            pltpu.VMEM((2 * TOK, HALF), BF16),
            pltpu.VMEM((TOK, HALF), BF16),
            pltpu.VMEM((TOK, HALF), BF16),
            pltpu.VMEM((2 * RANK, HALF), BF16),
            pltpu.VMEM((2 * RANK, HALF), BF16),
            pltpu.VMEM((32 * ROWS, HALF), BF16),
            pltpu.VMEM((ROWS, HALF), BF16),
            pltpu.VMEM((8, 128), F32),
            pltpu.VMEM((8, 128), F32),
            pltpu.VMEM((8, 8, 128), F32),
            pltpu.VMEM((8, 8, 128), F32),
            pltpu.VMEM((48, TOK), BF16),
            pltpu.VMEM((48, TOK), BF16),
            pltpu.VMEM((2, RANK, 2 * RANK), F32),
            pltpu.VMEM((RANK, 32 * ROWS), F32),
            pltpu.VMEM((32 * ROWS, 2 * RANK), BF16),
            pltpu.VMEM((32 * ROWS, 2 * TOK), F32),
            pltpu.VMEM((256, 2 * TOK), BF16),
            pltpu.VMEM((16, 2, 8, 128), F32),
            pltpu.VMEM((32, 8, 128), F32),
            pltpu.VMEM((1, TOK), jnp.int32),
            dma((11,)),
            dma((32, PARTS)),
            dma,
            dma((PARTS + 3,)),
            dma((3,)),
            dma((3,)),
            dma((3,)),
            dma,
            dma,
            pltpu.SemaphoreType.REGULAR((4,)),
        ],
        compiler_params=pltpu.CompilerParams(
            collective_id=0, has_side_effects=True, vmem_limit_bytes=64 * 1024 * 1024
        ),
        name="influence",
    )(x, g, members, queries.reshape(ROWS, WIDTH), down, up)
    return out.T


def solution(mesh):
    placed = (
        P("layer", "dp", None),
        P("layer", "dp", None),
        P("dp", None),
        P("layer", "dp", None, None, None),
        P("layer", None, None),
        P("layer", None, None),
    )
    return jax.shard_map(
        local, mesh=mesh, in_specs=placed, out_specs=P("dp", "layer"), check_vma=False
    )
```

```python
import math

import jax
import jax.numpy as jnp
from jax import lax
from jax.experimental import pallas as pl
from jax.experimental.pallas import tpu as pltpu
from jax.sharding import PartitionSpec as P

MESH = pl.DeviceIdType.MESH
F32 = jnp.float32
BF16 = jnp.bfloat16
HIGHEST = lax.Precision.HIGHEST
NT = (((1,), (1,)), ((), ()))
NN = (((1,), (0,)), ((), ()))

TOK = 256
WIDTH = 4096
HALF = WIDTH // 2
RANK = 16
TOKENS = 8192
ROWS = 16

PARTS = 2
SPAN = HALF // PARTS
SLOTS = tuple((dx, d) for dx in (0, 1) for d in (0, 1, -1, 2, -2, 3, -3, 4))
SLOT = {slot: i for i, slot in enumerate(SLOTS)}

GROUPS = (
    ((0, 0, 0), (0, 0, 1), (0, 1, 0), (0, -1, 0), (1, 0, 0), (0, 1, 1), (0, -1, 1), (1, 0, 1),
     (0, 2, 0), (0, -2, 0), (1, -1, 0), (0, 2, 1), (0, -2, 1), (1, 1, 0), (1, -1, 1), (0, -3, 0),
     (1, 1, 1), (0, 3, 0), (0, -3, 1), (1, 2, 1), (1, 2, 0), (1, -2, 0), (0, 3, 1), (1, -2, 1)),
    ((0, 4, 0), (0, 4, 1), (1, -3, 1), (1, 3, 1), (1, -3, 0), (1, 3, 0), (1, 4, 0), (1, 4, 1)),
)
ORDER = tuple(query for group in GROUPS for query in group)
POS = {query: i for i, query in enumerate(ORDER)}

STEPS = (
    (0, 0, 0, 0), (0, 0, 0, 0, "+"), (0, 0, 0, 0, "-"), (0, 0, 0, 1), (0, 0, 0, 0, "x"), (0, 0, 0, 1, "+"),
    (0, 0, 0, 1, "x"), (0, 0, 0, 1, "-"), (0, 0, 1, 0), (0, 0, 1, 1), (0, 0, 1, 1, "x"), (0, 0, 1, 0, "-"),
    (0, 0, 1, 1, "+"), ("gproj",), (0, 0, 1, 0, "+"), (0, 0, 1, 1, "-"), ("aproj",), ("moments",), ("known",),
    (0, 0, 1, 0, "x"), (0, 1, 0, 0), (0, -1, 0, 0), (0, -1, 0, 0, "-"), (0, -1, 0, 0, "x"), (0, 1, 0, 0, "+"),
    (1, 0, 0, 0), (0, -1, 0, 1), (0, -1, 0, 1, "-"), (1, 0, 0, 0, "+"), (0, -1, 0, 1, "x"), (0, 1, 0, 1),
    (0, 1, 0, 1, "x"), (0, 1, 1, 1), (0, -1, 1, 0), (0, -1, 1, 0, "-"), (0, 1, 1, 1, "+"), (0, -1, 1, 1),
    (1, 0, 0, 1), (0, 1, 1, 0), (0, 1, 0, 1, "+"), (1, 0, 1, 1), (0, 1, 1, 0, "+"), (1, 0, 1, 1, "+"),
    (0, -1, 1, 1, "x"), (0, -1, 1, 1, "-"), (0, -2, 0, 0), (0, -2, 0, 0, "-"), (0, 2, 0, 0), ("sides",),
    (0, 1, 1, 0, "x"), ("pair",), (0, 2, 0, 0, "+"), (0, -1, 1, 0, "x"), (0, -2, 0, 1), (0, -2, 0, 1, "-"),
    (0, -2, 1, 0), (0, -2, 1, 0, "-"), (0, 2, 1, 1), (0, 2, 1, 1, "x"), (1, -1, 0, 0), (1, -1, 0, 0, "-"),
    (1, 1, 0, 0), (1, 1, 0, 0, "+"), ("onehot",), (0, -2, 1, 0, "x"), (0, 2, 0, 1), (0, -2, 1, 1), (0, -2, 1, 1, "-"),
    (0, 2, 0, 1, "+"), (0, 2, 1, 0), (0, 2, 1, 0, "x"), (0, 2, 1, 0, "+"), (0, 2, 1, 1, "+"), (0, -3, 0, 0),
    (0, -3, 0, 0, "-"), (1, -1, 1, 1), (0, -3, 0, 1), (0, -3, 0, 1, "x"), (1, 1, 0, 1), (1, -1, 0, 1), (1, 0, 1, 0),
    (1, -1, 1, 1, "-"), (1, 1, 0, 1, "+"), (1, -1, 0, 1, "-"), (0, -3, 0, 1, "-"), (0, -3, 1, 0), (0, -3, 1, 0, "x"),
    (1, -1, 1, 0), (1, 1, 1, 0), (1, 2, 1, 1), (1, 2, 1, 1, "+"), (0, 3, 0, 0), (1, -2, 0, 0), (0, 3, 0, 1),
    (0, 3, 0, 1, "x"), (1, -2, 0, 0, "-"), (0, -3, 1, 1), (0, -3, 1, 1, "x"), (1, 2, 0, 0), (1, 2, 0, 0, "+"),
    (1, 2, 1, 0), (0, 3, 1, 0), ("across",), (0, -3, 1, 1, "-"), (0, 4, 0, 0), (1, -2, 1, 0), (0, 4, 0, 0, "x"),
    (0, 3, 1, 0, "+"), ("products", 0, 0, 1, "g"), ("products", 0, 0, 1, "x"), (1, 2, 1, 0, "+"), (1, -3, 0, 1),
    (1, -3, 0, 1, "-"), ("eliminate", 0), (0, 3, 1, 1), (1, 1, 1, 1), (1, -2, 0, 1), (1, -2, 1, 1), (1, 2, 0, 1),
    (1, -3, 1, 0), (1, -3, 1, 0, "-"), (1, 3, 1, 1), (1, 3, 1, 1, "+"), ("eliminate", 1), ("products", 0, 1, 2, "x"),
    ("products", 0, 1, 2, "g"), ("eliminate", 2), ("eliminate", 3), (0, 4, 1, 0), (1, -3, 0, 0), (0, 4, 1, 1),
    (1, 3, 0, 1), ("solve",), (1, 3, 0, 0), ("scores", 0), (1, 4, 1, 0), (0, 4, 0, 1), (1, 3, 1, 0), (1, 4, 0, 0),
    ("products", 1, 0, 1, "x"), (1, 4, 0, 1), (1, 4, 1, 1), (1, -3, 1, 1), ("products", 1, 0, 1, "g"),
    ("products", 1, 1, 2, "x"), ("products", 1, 1, 2, "g"), ("scores", 1),
)

def moved(query, way):
    dx, d, p = query
    if way == "x":
        return (1 - dx, d, p)
    d = d + 1 if way == "+" else d - 1
    return (dx, 4 if d == -4 else d, p)


def dot(a, b, dims, precision=None):
    return lax.dot_general(a, b, dims, precision=precision, preferred_element_type=F32)


def kernel(
    x_ref, g_ref, member_ref, query_ref, down_ref, up_ref, out_ref,
    xb, gb, xo, go, fm, fo, q, qo, mine, theirs, pm, ps, pown, psib,
    work, rall, vb, kst, onehot, so, rx,
    mem, load_sem, piece_sem, send_sem, side_send, side_recv, msg_send, msg_recv, fin_send, fin_recv, known,
):
    layer, block = lax.axis_index("layer"), lax.axis_index("dp")
    xh, y, core = block // 16, (block // 2) % 8, block % 2
    z, xl = layer // 2, layer % 2

    def along_y(n):
        return (layer, xh * 16 + ((y + n + 8) % 8) * 2 + core)

    def along_z(n):
        return (((z + n + 8) % 8) * 2 + xl, block)

    partner = (layer, (1 - xh) * 16 + y * 2 + core)
    sibling = (layer, xh * 16 + y * 2 + (1 - core))
    beside = (z * 2 + (1 - xl), block)
    ways = {"+": along_y(1), "-": along_y(-1), "x": partner}

    def remote(src, dst, ssem, rsem, device):
        return pltpu.make_async_remote_copy(
            src_ref=src, dst_ref=dst, send_sem=ssem, recv_sem=rsem, device_id=device, device_id_type=MESH
        )

    def signal(sem, device):
        pl.semaphore_signal(sem, inc=1, device_id=device, device_id_type=MESH)

    def rows(piece):
        return pl.ds(POS[piece] * ROWS, ROWS)

    here = pl.ds(pl.multiple_of(core * HALF, HALF), HALF)
    there = pl.ds(pl.multiple_of((1 - core) * HALF, HALF), HALF)

    near = (
        along_y(1), along_y(-1), partner, sibling, beside, along_z(1), along_z(-1),
    )
    barrier = pltpu.get_barrier_semaphore()
    for device in near:
        signal(barrier, device)

    loads = [
        pltpu.make_async_copy(query_ref.at[:, here], q.at[rows((0, 0, 0))], load_sem.at[0]),
        pltpu.make_async_copy(query_ref.at[:, there], qo, load_sem.at[1]),
        pltpu.make_async_copy(up_ref.at[0, :, here], fm.at[pl.ds(0, RANK)], load_sem.at[2]),
        pltpu.make_async_copy(up_ref.at[0, :, there], fo.at[pl.ds(0, RANK)], load_sem.at[3]),
        pltpu.make_async_copy(down_ref.at[0, :, here], fm.at[pl.ds(RANK, RANK)], load_sem.at[4]),
        pltpu.make_async_copy(down_ref.at[0, :, there], fo.at[pl.ds(RANK, RANK)], load_sem.at[5]),
        pltpu.make_async_copy(g_ref.at[0, :, here], gb.at[pl.ds(0, TOK)], load_sem.at[6]),
        pltpu.make_async_copy(g_ref.at[0, :, there], go, load_sem.at[7]),
        pltpu.make_async_copy(x_ref.at[0, :, here], xb.at[pl.ds(0, TOK)], load_sem.at[8]),
        pltpu.make_async_copy(x_ref.at[0, :, there], xo, load_sem.at[9]),
        pltpu.make_async_copy(member_ref, mem, load_sem.at[10]),
    ]
    for copy in loads:
        copy.start()
    so[...] = jnp.zeros(so.shape, F32)
    loads[0].wait()
    loads[1].wait()

    pl.semaphore_wait(barrier, len(near))

    def part(query, h):
        return q.at[rows(query), pl.ds(h * SPAN, SPAN)]

    def passed_on(query, h, way):
        target = moved(query, way)
        remote(
            part(query, h), part(target, h), send_sem, piece_sem.at[POS[target], h], ways[way]
        ).start()

    def landed(query, h):
        if query == (0, 0, 1):
            side[h].wait_recv()
        elif query != (0, 0, 0):
            remote(part(query, h), part(query, h), send_sem, piece_sem.at[POS[query], h], partner).wait_recv()

    side = [
        remote(
            qo.at[:, pl.ds(h * SPAN, SPAN)], part((0, 0, 1), h), side_send.at[h], piece_sem.at[POS[(0, 0, 1)], h], sibling
        )
        for h in range(PARTS)
    ]
    rest = [
        remote(go, gb.at[pl.ds(TOK, TOK)], side_send.at[PARTS], side_recv.at[0], sibling),
        remote(xo, xb.at[pl.ds(TOK, TOK)], side_send.at[PARTS + 1], side_recv.at[1], sibling),
        remote(pown, psib, side_send.at[PARTS + 2], side_recv.at[2], sibling),
    ]
    to_partner = remote(mine, theirs, msg_send.at[0], msg_recv.at[0], partner)
    pair = [remote(pm.at[0], pm.at[n], msg_send.at[1], msg_recv.at[1], along_y(n)) for n in range(1, 8)]
    pairs = remote(pm.at[pl.ds(1, 7)], pm.at[pl.ds(1, 7)], msg_send.at[1], msg_recv.at[1], sibling)
    across = remote(pm, ps, msg_send.at[2], msg_recv.at[2], sibling)

    def step_gproj():
        for copy in loads[2:8]:
            copy.wait()
        rest[0].start()
        projections["own"] = dot(fm[...], q[rows((0, 0, 0)), :], NT) + dot(fo[...], qo[...], NT)
        projections["grad"] = dot(fm[0:RANK, :], gb[0:TOK, :], NT) + dot(fo[0:RANK, :], go[...], NT)

    def step_aproj():
        loads[8].wait()
        loads[9].wait()
        rest[1].start()
        projections["act"] = dot(fm[RANK:, :], xb[0:TOK, :], NT) + dot(fo[RANK:, :], xo[...], NT)

    def step_moments():
        own_q = projections["own"]
        query_proj = jnp.concatenate([own_q[0:RANK, 8:16], own_q[RANK:, 0:8]], axis=1)
        proj = jnp.concatenate([projections["grad"], projections["act"]], axis=0)
        cov = dot(proj, proj, NT, HIGHEST)
        both = jnp.concatenate(
            [cov[0:RANK, 0:RANK], cov[RANK:, RANK:], query_proj, jnp.zeros((RANK, 16), F32)], axis=1
        )
        mine[...] = jnp.concatenate([both[0:8], both[8:16]], axis=1)
        to_partner.start()
        loads[10].wait()
        pown[0:32, :] = proj.astype(BF16)
        pown[32:48, :] = jnp.broadcast_to(mem[...].astype(F32), (16, TOK)).astype(BF16)
        rest[2].start()

    def step_known():
        pl.semaphore_wait(known.at[0], 4)
        for device in (along_y(2), along_y(-2), along_z(2), along_z(-2)):
            signal(known.at[1], device)

    def step_pair():
        pl.semaphore_wait(known.at[1], 4)
        signal(known.at[2], beside)
        to_partner.wait_recv()
        lane = lax.broadcasted_iota(jnp.int32, (8, 128), 1) % 64
        from_x = theirs[...]
        own = mine[...]
        pm[0] = jnp.where(lane < 32, own + from_x, jnp.where(lane < 48, own, pltpu.roll(from_x, 16, 1)))
        for copy in pair:
            copy.start()

    def step_across():
        pl.semaphore_wait(known.at[2], 1)
        signal(known.at[3], sibling)
        pairs.wait_recv()
        across.start()

    def step_onehot():
        rest[2].wait_recv()
        example = lax.broadcasted_iota(jnp.int32, (128, TOK), 0)
        onehot[0:128, 0:TOK] = (example == mem[...]).astype(F32).astype(BF16)
        onehot[0:128, TOK:] = jnp.zeros((128, TOK), BF16)
        onehot[128:, 0:TOK] = jnp.zeros((128, TOK), BF16)
        others = psib[32:48, :].astype(F32)[0:1, :]
        onehot[128:, TOK:] = (example.astype(F32) == others).astype(F32).astype(BF16)

    def step_sides():
        rest[0].wait_recv()
        rest[1].wait_recv()

    def span(index):
        first = POS[GROUPS[index][0]] * ROWS
        return first, len(GROUPS[index]) * ROWS

    def step_products(index, begin, end, operand):
        first, count = span(index)
        columns = slice(begin * SPAN, end * SPAN)
        rows_of, lift = (xb, 0) if operand == "x" else (gb, 8)
        found = dot(q[first:first + count, columns], rows_of[:, columns], NT)
        for i in range(lift, count, ROWS):
            if begin == 0:
                kst[first + i:first + i + 8, :] = found[i:i + 8]
            else:
                kst[first + i:first + i + 8, :] += found[i:i + 8]

    def step_eliminate(quarter):
        if quarter == 0:
            across.wait_recv()
            total = pm[0] + ps[0]
            for n in range(1, 8):
                total = total + (pm[n] + ps[n])
            moments = jnp.concatenate([total[:, 0:32], total[:, 64:96]], axis=0) * (1.0 / TOKENS)
            for i, (dx, d, p) in enumerate(ORDER):
                source = (ps if p else pm)[(d + 8) % 8]
                at = 32 + 16 * dx
                rall[0:8, 16 * i:16 * i + 16] = source[:, at:at + 16]
                rall[8:16, 16 * i:16 * i + 16] = source[:, at + 64:at + 80]
            diagonal = (
                lax.broadcasted_iota(jnp.int32, (RANK, RANK), 0) == lax.broadcasted_iota(jnp.int32, (RANK, RANK), 1)
            ).astype(F32)
            for i in (0, 1):
                moment = moments[:, RANK * i:RANK * (i + 1)]
                trace = jnp.sum(jnp.sum(moment * diagonal, axis=1, keepdims=True), axis=0, keepdims=True)
                scales.append(1.0 / trace)
                work[i] = jnp.concatenate([moment * scales[i] + (0.1 / RANK) * diagonal, diagonal], axis=1)
        row = lax.broadcasted_iota(jnp.int32, (RANK, 2 * RANK), 0)
        tables = [work[0], work[1]]
        for k in range(4 * quarter, 4 * quarter + 4):
            for i in (0, 1):
                table = tables[i]
                pivot = table[k:k + 1, :] / table[k:k + 1, k:k + 1]
                tables[i] = jnp.where(row == k, pivot, table - table[:, k:k + 1] * pivot)
        work[0] = tables[0]
        work[1] = tables[1]

    def step_solve():
        kind = lax.broadcasted_iota(jnp.int32, (RANK, 32 * ROWS), 1) % ROWS
        solved_grad = dot(work[0][:, RANK:], rall[...] * scales[0], NN, HIGHEST)
        solved_act = dot(work[1][:, RANK:], rall[...] * scales[1], NN, HIGHEST)
        solved = jnp.concatenate(
            [jnp.where(kind < 8, solved_grad, 0.0), jnp.where(kind < 8, 0.0, solved_act)], axis=0
        )
        vb[...] = solved.T.astype(BF16)
        pl.semaphore_wait(known.at[3], 1)

    def step_scores(index):
        first, count = span(index)
        group = GROUPS[index]
        both_proj = jnp.concatenate([pown[0:32, :], psib[0:32, :]], axis=1)
        weights = dot(vb[first:first + count, :], both_proj, NN)
        terms = (weights * kst[first:first + count, :]).reshape(len(group), ROWS, 2 * TOK)
        terms = jnp.sum(terms, axis=1)
        high = terms.astype(BF16)
        low = (terms - high.astype(F32)).astype(BF16)
        halves = dot(jnp.concatenate([high, low], axis=0), onehot[...], NT)
        sums = halves[:len(group)] + halves[len(group):]
        for i, (dx, d, p) in enumerate(group):
            for k in (0, 1):
                so[SLOT[dx, d], k, p:p + 1, :] = sums[i:i + 1, k * 128:(k + 1) * 128]
        done = {query for members in GROUPS[:index + 1] for query in members}
        before = {query for members in GROUPS[:index] for query in members}
        mate = xh * 16 + y * 2 + (1 - core)
        for slot in SLOTS:
            queries = {slot + (0,), slot + (1,)}
            if not queries <= done or queries <= before:
                continue
            dx, d = slot
            target = ((1 - xh) if dx else xh) * 8 + (y - d + 8) % 8
            step = (target - layer + 16) % 16

            @pl.when(step == 0)
            def _():
                rx[0] = so[SLOT[slot], 0]

            @pl.when(step != 0)
            def _():
                remote(so.at[SLOT[slot], 0], rx.at[step * 2], fin_send, fin_recv, (target, block)).start()

            remote(so.at[SLOT[slot], 1], rx.at[step * 2 + 1], fin_send, fin_recv, (target, mate)).start()

    projections, scales = {}, []
    work_of = {
        "gproj": step_gproj, "aproj": step_aproj, "moments": step_moments, "known": step_known, "pair": step_pair,
        "across": step_across, "onehot": step_onehot, "sides": step_sides, "products": step_products,
        "eliminate": step_eliminate, "solve": step_solve, "scores": step_scores,
    }
    for copy in side:
        copy.start()
    for device in (along_y(1), along_y(-1), along_z(1), along_z(-1)):
        signal(known.at[0], device)
    for item in STEPS:
        if isinstance(item[0], str):
            work_of[item[0]](*item[1:])
        elif len(item) == 4:
            landed(item[:3], item[3])
        else:
            passed_on(item[:3], item[3], item[4])

    tail = rx.at[pl.ds(1, 31)]
    remote(tail, tail, fin_send, fin_recv, sibling).wait()
    same, other = rx[0], rx[1]
    for i in range(1, 16):
        same = same + rx[2 * i]
        other = other + rx[2 * i + 1]
    first = same[0:1, 0:32] + other[1:2, 0:32]
    second = same[1:2, 0:32] + other[0:1, 0:32]
    scale = 1.0 / (8.0 * math.sqrt(2.0 * RANK * WIDTH * 16))
    out_ref[0:1, :] = jnp.where(core == 0, first, second) * scale
    out_ref[1:2, :] = jnp.where(core == 0, second, first) * scale

    sent = q.at[pl.ds(0, 30 * ROWS)]
    remote(sent, sent, send_sem, piece_sem.at[0, 0], partner).wait_send()
    for copy in side + rest:
        copy.wait_send()
    to_partner.wait_send()
    pairs.wait_send()
    across.wait_send()


def local(x, g, members, queries, down, up):
    hbm = pl.BlockSpec(memory_space=pltpu.HBM)
    vmem = pl.BlockSpec(memory_space=pltpu.VMEM)
    dma = pltpu.SemaphoreType.DMA
    out = pl.pallas_call(
        kernel,
        out_shape=jax.ShapeDtypeStruct((2, 32), F32),
        in_specs=[hbm] * 6,
        out_specs=vmem,
        scratch_shapes=[
            pltpu.VMEM((2 * TOK, HALF), BF16),
            pltpu.VMEM((2 * TOK, HALF), BF16),
            pltpu.VMEM((TOK, HALF), BF16),
            pltpu.VMEM((TOK, HALF), BF16),
            pltpu.VMEM((2 * RANK, HALF), BF16),
            pltpu.VMEM((2 * RANK, HALF), BF16),
            pltpu.VMEM((32 * ROWS, HALF), BF16),
            pltpu.VMEM((ROWS, HALF), BF16),
            pltpu.VMEM((8, 128), F32),
            pltpu.VMEM((8, 128), F32),
            pltpu.VMEM((8, 8, 128), F32),
            pltpu.VMEM((8, 8, 128), F32),
            pltpu.VMEM((48, TOK), BF16),
            pltpu.VMEM((48, TOK), BF16),
            pltpu.VMEM((2, RANK, 2 * RANK), F32),
            pltpu.VMEM((RANK, 32 * ROWS), F32),
            pltpu.VMEM((32 * ROWS, 2 * RANK), BF16),
            pltpu.VMEM((32 * ROWS, 2 * TOK), F32),
            pltpu.VMEM((256, 2 * TOK), BF16),
            pltpu.VMEM((16, 2, 8, 128), F32),
            pltpu.VMEM((32, 8, 128), F32),
            pltpu.VMEM((1, TOK), jnp.int32),
            dma((11,)),
            dma((32, PARTS)),
            dma,
            dma((PARTS + 3,)),
            dma((3,)),
            dma((3,)),
            dma((3,)),
            dma,
            dma,
            pltpu.SemaphoreType.REGULAR((4,)),
        ],
        compiler_params=pltpu.CompilerParams(
            collective_id=0, has_side_effects=True, vmem_limit_bytes=64 * 1024 * 1024
        ),
        name="influence",
    )(x, g, members, queries.reshape(ROWS, WIDTH), down, up)
    return out.T


def solution(mesh):
    placed = (
        P("layer", "dp", None),
        P("layer", "dp", None),
        P("dp", None),
        P("layer", "dp", None, None, None),
        P("layer", None, None),
        P("layer", None, None),
    )
    return jax.shard_map(
        local, mesh=mesh, in_specs=placed, out_specs=P("dp", "layer"), check_vma=False
    )
```
